32 devices in a mesh: chan: 8 (over z, x), hour: 4 (over y, core).
Axes of the slice: x: 2, y: 2, z: 4, core: 2. Of those that a mesh axis runs over, the one named last changes fastest.
Arguments:
- traces: bfloat16 [1024, 16384], P('chan', 'hour'), may hold values from -6 to 6
- taps: bfloat16 [1024, 512], P('chan'), may hold values from -0.25 to 0.25
- bin_ids: int32 [4, 8], P(None, 'chan'), may hold values from 0 to 31
- owners: int32 [32], replicated, may hold values from 0 to 31, each once
Outputs:
- stacks: float32 [32, 8192], P(('chan', 'hour'))
The draws below stay inside these ranges and needn't reach their ends.
Inputs may be any that keep to these rules, and one draw needn't show every extreme that they name: bin_ids[r, i] is the distance bin of the pair of block i - r - 1 with block i; entries with i <= r name no pair and are not read. owners is a permutation: bin b is held in row owners[b] of stacks.
All inputs are finite; a program needn't handle non-finite values.
Results may differ from the reference program's by a relative error of at most 0.004.
Values may be sent and summed in bfloat16 or wider, within the bound.
A program may use at most 256 MiB of HBM per device.

```python
import math
import jax
import jax.numpy as jnp
from jax import lax

CB = 128
FR = 4096
TAPS = 512
FRAMES = 1
ROUNDS = 4
BLOCKS = 8
NCH = 1024
TIME = 16384
NBINS = 32
N_CHAN = 8
N_HOUR = 4


def with_ends(array, key, least, top_value):
    dims = array.shape
    place = [jax.random.randint(jax.random.fold_in(key, axis), (), 0, dims[axis]) for axis in range(len(dims))]
    array = array.at[tuple(place)].set(least)
    longest = dims.index(max(dims))
    place[longest] = (place[longest] + 1) % dims[longest]
    return array.at[tuple(place)].set(top_value)


def level_of(key, extent, shards, low, largest):
    loudness, own = 1.0, jax.random.fold_in(key, 6)
    for dim, shards_of in shards:
        steps = jnp.exp(jax.random.uniform(jax.random.fold_in(own, dim), (shards_of,), jnp.float32, low / len(shards), largest / len(shards)))
        loudness = loudness * jnp.repeat(steps, extent[dim] // shards_of).reshape([-1 if axis == dim else 1 for axis in range(len(extent))])
    return loudness


def bell_draw(key, extent, deviation, most, cuts=(), kind=jnp.bfloat16):
    entries = jax.random.normal(key, extent, jnp.float32) * deviation
    if len(cuts) > 0:
        entries = level_of(key, extent, cuts, -0.22, 0.18) * entries
    return jnp.clip(entries, min=-most, max=most).astype(kind)


def setup_inputs(seed: int = 0) -> dict:
    splits = jax.random.split(jax.random.key(seed), 5)
    return {
        "traces": bell_draw(splits[0], (NCH, TIME), 1.0, 6.0, ((0, 8), (1, 4))),
        "taps": bell_draw(splits[1], (NCH, TAPS), TAPS ** -0.5, 0.25, ((0, 8),)),
        "bin_ids": with_ends(jax.random.randint(splits[2], (ROUNDS, BLOCKS), 0, NBINS), jax.random.fold_in(splits[2], 1), 0, NBINS - 1).astype(jnp.int32),
        "owners": jax.random.permutation(splits[3], NBINS).astype(jnp.int32),
    }


def spectra(block, filters):
    signal = block.astype(jnp.float32).reshape(CB, N_HOUR * FRAMES, FR)
    freq = jnp.fft.rfft(signal, n=2 * FR, axis=-1)[..., :FR]
    response = jnp.fft.rfft(filters.astype(jnp.float32), n=2 * FR, axis=-1)[:, :FR]
    product = freq * response[:, None, :]
    return (jnp.real(product).astype(jnp.bfloat16), jnp.imag(product).astype(jnp.bfloat16))

def reference(traces, taps, bin_ids, owners):
    blocks = traces.reshape(N_CHAN, CB, N_HOUR * FRAMES * FR)
    filter_blocks = taps.reshape(N_CHAN, CB, TAPS)

    def pair_terms(block_index):
        own_re, own_im = spectra(blocks[block_index], filter_blocks[block_index])
        near_re = own_re.astype(jnp.float32)
        near_im = own_im.astype(jnp.float32)
        results = []
        for offset in range(ROUNDS):
            other = jnp.maximum(block_index - offset - 1, 0)
            far_re, far_im = spectra(blocks[other], filter_blocks[other])
            far_re = far_re.astype(jnp.float32)
            far_im = far_im.astype(jnp.float32)
            cross_re = lax.optimization_barrier(jnp.sum(far_re * near_re + far_im * near_im, axis=(0, 1)))
            cross_im = lax.optimization_barrier(jnp.sum(far_im * near_re - far_re * near_im, axis=(0, 1)))
            live = block_index >= offset + 1
            results.append(jnp.where(live, jnp.stack([cross_re, cross_im]), 0.0))
        return jnp.stack(results)
    cross = lax.map(pair_terms, jnp.arange(N_CHAN, dtype=jnp.int32))
    valid = jnp.arange(N_CHAN, dtype=jnp.int32)[:, None] >= jnp.arange(1, ROUNDS + 1, dtype=jnp.int32)[None, :]
    labels = jnp.where(valid, bin_ids.T, NBINS).reshape(-1).astype(jnp.int32)
    stack = jax.ops.segment_sum(cross.reshape(N_CHAN * ROUNDS, 2, FR), labels, num_segments=NBINS + 1)[:NBINS]
    placed = jnp.zeros_like(stack).at[owners].set(stack)
    spectrum = placed[:, 0] + 1j * placed[:, 1]
    padded = jnp.concatenate([spectrum, jnp.zeros((NBINS, 1), spectrum.dtype)], axis=1)
    scale = 1.0 / (FR * math.sqrt(FR * N_HOUR * FRAMES * CB))
    return (jnp.fft.irfft(padded, n=2 * FR, axis=-1) * (2 * FR * scale)).astype(jnp.float32)
```

```python
import functools
import math

import jax
import jax.numpy as jnp
import numpy as np
from jax import lax
from jax.experimental import pallas as pl
from jax.experimental.pallas import tpu as pltpu
from jax.sharding import PartitionSpec as P

FR = 4096
ROUNDS = 4
MESH = pl.DeviceIdType.MESH


exact = lax.Precision.HIGHEST

def passed_along(shard, axis, by):
    devices = lax.axis_size(axis)
    pairs = [(i, i + by) for i in range(devices) if 0 <= i + by < devices]
    return lax.ppermute(shard, axis, pairs)


def transform(real_part, imag_part, count):
    span = real_part.shape[-1]
    inner = 2 * span // 128
    lead = real_part.shape[:-1]
    first = jnp.arange(64, dtype=jnp.float32)[:, None]
    middle = jnp.arange(128, dtype=jnp.float32)[None, :]
    angle_one = 2.0 * math.pi / 128.0 * jnp.mod(first * middle, 128.0)
    cos_one = jnp.cos(angle_one)
    sin_one = -jnp.sin(angle_one)
    second = jnp.arange(inner, dtype=jnp.float32)[:, None]
    angle_turn = 2.0 * math.pi / (128.0 * inner) * jnp.mod(second * middle, 128.0 * inner)
    cos_turn = jnp.cos(angle_turn)
    sin_turn = -jnp.sin(angle_turn)
    outer = jnp.arange(count // 128, dtype=jnp.float32)[None, :]
    angle_two = 2.0 * math.pi / inner * jnp.mod(second * outer, float(inner))
    cos_two = jnp.cos(angle_two)
    sin_two = -jnp.sin(angle_two)
    grid = real_part.reshape(lead + (64, inner))
    section_re = jnp.einsum("...an,ak->...nk", grid, cos_one, precision=exact)
    section_im = jnp.einsum("...an,ak->...nk", grid, sin_one, precision=exact)
    if imag_part is not None:
        grid_im = imag_part.reshape(lead + (64, inner))
        section_re = section_re - jnp.einsum("...an,ak->...nk", grid_im, sin_one, precision=exact)
        section_im = section_im + jnp.einsum("...an,ak->...nk", grid_im, cos_one, precision=exact)
    turned_re = section_re * cos_turn - section_im * sin_turn
    turned_im = section_re * sin_turn + section_im * cos_turn
    out_re = jnp.einsum("...nk,nm->...mk", turned_re, cos_two, precision=exact) - jnp.einsum(
        "...nk,nm->...mk", turned_im, sin_two, precision=exact
    )
    out_im = jnp.einsum("...nk,nm->...mk", turned_re, sin_two, precision=exact) + jnp.einsum(
        "...nk,nm->...mk", turned_im, cos_two, precision=exact
    )
    return (out_re.reshape(lead + (count,)), out_im.reshape(lead + (count,)))


def filtered(samples, filters):
    channels = samples.shape[0]
    frames = samples.shape[1] // FR
    signal = samples.astype(jnp.float32).reshape(channels, frames, FR)
    freq_re, freq_im = transform(signal, None, FR)
    padded_taps = jnp.pad(filters.astype(jnp.float32), ((0, 0), (0, FR - filters.shape[1])))
    resp_re, resp_im = transform(padded_taps, None, FR)
    resp_re = resp_re[:, None, :]
    resp_im = resp_im[:, None, :]
    spec_re = (freq_re * resp_re - freq_im * resp_im).astype(jnp.bfloat16)
    spec_im = (freq_re * resp_im + freq_im * resp_re).astype(jnp.bfloat16)
    return (spec_re, spec_im)


def body(traces, taps, bin_ids, owners):
    channels = traces.shape[0]
    frames = traces.shape[1] // FR
    spec_re, spec_im = filtered(traces, taps)
    mine = lax.axis_index("chan")
    near_re = spec_re.astype(jnp.float32)
    near_im = spec_im.astype(jnp.float32)
    results = []
    for offset in range(ROUNDS):
        far_re, far_im = passed_along((spec_re, spec_im), "chan", offset + 1)
        far_re = far_re.astype(jnp.float32)
        far_im = far_im.astype(jnp.float32)
        cross_re = jnp.sum(far_re * near_re + far_im * near_im, axis=(0, 1))
        cross_im = jnp.sum(far_im * near_re - far_re * near_im, axis=(0, 1))
        results.append(jnp.stack([cross_re, cross_im]))
    contrib = jnp.stack(results)
    nbins = owners.shape[0]
    own_bins = bin_ids[:, 0]
    labels = jnp.arange(nbins, dtype=jnp.int32)
    places = jnp.sum(jnp.where(own_bins[:, None] == labels[None, :], owners[None, :], 0), axis=1)
    valid = jnp.arange(ROUNDS, dtype=jnp.int32) < mine
    places = jnp.where(valid, places, -1)
    width = contrib.shape[2]
    flat = contrib.reshape(ROUNDS, 2 * width)
    per_device = nbins // lax.axis_size("chan")
    rows = jnp.arange(lax.axis_size("chan") * per_device, dtype=jnp.int32)
    onehot = (places[None, :] == rows[:, None]).astype(jnp.float32)
    stacked = lax.psum_scatter(
        jnp.dot(onehot, flat, precision=exact, preferred_element_type=jnp.float32),
        "chan",
        scatter_dimension=0,
        tiled=True,
    )
    stacked = stacked.reshape(per_device, 2, width)
    final = lax.psum_scatter(stacked, "hour", scatter_dimension=0, tiled=True)
    weights = jnp.where(jnp.arange(FR) == 0, 1.0, 2.0).astype(jnp.float32)
    wave_re, wave_im = transform(final[:, 0] * weights, -final[:, 1] * weights, 2 * FR)
    norm = 1.0 / (FR * math.sqrt(FR * lax.axis_size("hour") * frames * channels))
    return wave_re * norm

SPLIT = 8
SUB = FR // SPLIT
LANES = 128
TILES = SUB // LANES


def sub_tables():
    a = np.arange(SUB)[:, None]
    k1 = np.arange(SUB)[None, :]
    turn = 2.0 * np.pi * ((a * k1) % (2 * SUB)) / (2 * SUB)
    cos, sin = np.cos(turn), -np.sin(turn)
    sin[:, 0] = 1.0 - 2.0 * (np.arange(SUB) % 2)
    table = np.stack([cos.reshape(SUB, TILES, LANES), sin.reshape(SUB, TILES, LANES)], axis=2)
    return table.reshape(SUB, 2 * SUB)


def two_parts(table):
    high = table.astype(jnp.bfloat16)
    low = (table - high.astype(np.float64)).astype(jnp.bfloat16)
    return high, low


def pick_table():
    span = SPLIT * LANES
    table = np.zeros((span, span), np.float32)
    for n in range(SPLIT):
        for b in range(LANES):
            table[SPLIT * b + n, n * LANES + b] = 1.0
    return table.astype(jnp.bfloat16)


def turn_table():
    n = np.arange(SPLIT)[:, None]
    k1 = np.arange(SUB)[None, :]
    turn = 2.0 * np.pi * n * k1 / (2 * FR)
    table = np.stack([np.cos(turn), -np.sin(turn)], axis=1).reshape(SPLIT, 2, TILES, 1, LANES)
    table = np.broadcast_to(table.transpose(2, 0, 1, 3, 4), (TILES, SPLIT, 2, 8, LANES))
    return np.ascontiguousarray(table).astype(np.float32)


def times(value, angle):
    re, im = value
    c, s = math.cos(angle), math.sin(angle)
    if abs(s) < 1e-12:
        return (re, im) if c > 0 else (-re, -im)
    if abs(c) < 1e-12:
        return (-im, re) if s > 0 else (im, -re)
    if abs(abs(c) - abs(s)) < 1e-12:
        root = abs(c)
        p, q = math.copysign(1.0, c), math.copysign(1.0, s)
        first = (re if p > 0 else -re) + (-im if q > 0 else im)
        second = (re if q > 0 else -re) + (im if p > 0 else -im)
        return first * root, second * root
    return re * c - im * s, re * s + im * c


def small_dft(values, sign, half=False):
    size = len(values)
    if size == 1:
        return values
    even = small_dft(values[0::2], sign)
    odd = small_dft(values[1::2], sign)
    low, high = [], []
    for k in range(size // 2):
        turned = times(odd[k], sign * 2.0 * math.pi * k / size)
        low.append((even[k][0] + turned[0], even[k][1] + turned[1]))
        if not half:
            high.append((even[k][0] - turned[0], even[k][1] - turned[1]))
    return low + high


def pairs_of(blocks):
    return [(r, i) for r in range(ROUNDS) for i in range(blocks) if i >= r + 1]


def correlate_kernel(blocks, x, taps, pick, high, low, turns, onehot, out, xd, td, fx, fh, spec, cross):
    rows = x.shape[0]
    per = rows // blocks
    span = SPLIT * LANES
    for q in range(FR // span):
        part = jnp.dot(
            x[:, q * span : (q + 1) * span], pick[...], preferred_element_type=jnp.float32
        ).astype(jnp.bfloat16)
        for n in range(SPLIT):
            xd[n, :, q * LANES : (q + 1) * LANES] = part[:, n * LANES : (n + 1) * LANES]
    count = taps.shape[1]
    part = jnp.dot(taps[...], pick[:count, :], preferred_element_type=jnp.float32).astype(jnp.bfloat16)
    for n in range(SPLIT):
        td[n] = part[:, n * LANES : (n + 1) * LANES]

    @pl.loop(0, SPLIT)
    def _(n):
        fx[n] = jnp.dot(xd[n], high[...], preferred_element_type=jnp.float32) + jnp.dot(
            xd[n], low[...], preferred_element_type=jnp.float32
        )
        fh[n] = jnp.dot(td[n], high[:LANES, :], preferred_element_type=jnp.float32) + jnp.dot(
            td[n], low[:LANES, :], preferred_element_type=jnp.float32
        )

    pairs = pairs_of(blocks)
    lane0 = lax.broadcasted_iota(jnp.int32, (8, LANES), 1) == 0
    for t in range(TILES):

        @pl.loop(0, rows // 8)
        def _(g):
            here = pl.ds(pl.multiple_of(8 * g, 8), 8)

            def bins_of(f):
                values, extra = [], []
                for n in range(SPLIT):
                    re = f[n, here, 2 * t * LANES : (2 * t + 1) * LANES]
                    im = f[n, here, (2 * t + 1) * LANES : (2 * t + 2) * LANES]
                    if t == 0:
                        angle = -math.pi * n / SPLIT
                        extra.append((im * math.cos(angle), im * math.sin(angle)))
                        im = jnp.where(lane0, 0.0, im)
                    if n == 0:
                        values.append((re, im))
                    else:
                        c, s = turns[t, n, 0], turns[t, n, 1]
                        values.append((re * c - im * s, re * s + im * c))
                found = small_dft(values, -1)
                if t == 0:
                    more = small_dft(extra, -1, half=True)
                    for k2 in range(SPLIT // 2):
                        old = found[SPLIT // 2 + k2]
                        found[SPLIT // 2 + k2] = tuple(
                            jnp.where(lane0, more[k2][z], old[z]) for z in range(2)
                        )
                return found

            freq = bins_of(fx)
            resp = bins_of(fh)
            for k2 in range(SPLIT):
                (xr, xi), (hr, hi) = freq[k2], resp[k2]
                spec[k2, 0, here, :] = (xr * hr - xi * hi).astype(jnp.bfloat16).astype(jnp.float32)
                spec[k2, 1, here, :] = (xr * hi + xi * hr).astype(jnp.bfloat16).astype(jnp.float32)

        @pl.loop(0, SPLIT)
        def _(k2):
            for p, (r, i) in enumerate(pairs):
                re = im = None
                for c in range(per // 8):
                    near = pl.ds(i * per + 8 * c, 8)
                    far = pl.ds((i - r - 1) * per + 8 * c, 8)
                    nr, ni = spec[k2, 0, near, :], spec[k2, 1, near, :]
                    fr, fi = spec[k2, 0, far, :], spec[k2, 1, far, :]
                    one, two = fr * nr + fi * ni, fi * nr - fr * ni
                    re, im = (one, two) if re is None else (re + one, im + two)
                cross[8 * p : 8 * p + 8, :LANES] = re
                cross[8 * p : 8 * p + 8, LANES:] = im
            total = cross[...]
            top = total.astype(jnp.bfloat16)
            rest = (total - top.astype(jnp.float32)).astype(jnp.bfloat16)
            place = pl.multiple_of((t * SPLIT + k2) * 2 * LANES, 2 * LANES)
            out[:, pl.ds(place, 2 * LANES)] = jnp.dot(
                onehot[...], top, preferred_element_type=jnp.float32
            ) + jnp.dot(onehot[...], rest, preferred_element_type=jnp.float32)


def correlate(x, taps, onehot, blocks):
    rows = x.shape[0]
    high, low = two_parts(sub_tables())
    nbins, depth = onehot.shape
    vmem = pl.BlockSpec(memory_space=pltpu.VMEM)
    return pl.pallas_call(
        functools.partial(correlate_kernel, blocks),
        out_shape=jax.ShapeDtypeStruct((nbins, 2 * FR), jnp.float32),
        in_specs=[vmem] * 7,
        out_specs=vmem,
        scratch_shapes=[
            pltpu.VMEM((SPLIT, rows, SUB), jnp.bfloat16),
            pltpu.VMEM((SPLIT, rows, LANES), jnp.bfloat16),
            pltpu.VMEM((SPLIT, rows, 2 * SUB), jnp.float32),
            pltpu.VMEM((SPLIT, rows, 2 * SUB), jnp.float32),
            pltpu.VMEM((SPLIT, 2, rows, LANES), jnp.float32),
            pltpu.VMEM((depth, 2 * LANES), jnp.float32),
        ],
        compiler_params=pltpu.CompilerParams(vmem_limit_bytes=48 * 2**20),
    )(x, taps, jnp.asarray(pick_table()), jnp.asarray(high), jnp.asarray(low), jnp.asarray(turn_table()), onehot)


def wave_of(row, norm):
    tiles = row.reshape(TILES, SPLIT, 2, LANES).transpose(2, 1, 0, 3).reshape(2, SPLIT, SUB)
    weight = np.full((SPLIT, SUB), 2.0)
    weight[0, 0] = 1.0
    tiles = tiles * jnp.asarray(weight.astype(np.float32) * np.float32(norm))
    main = np.ones((SPLIT, SUB))
    main[SPLIT // 2 :, 0] = 0.0
    re, im = tiles[0] * main.astype(np.float32), tiles[1] * main.astype(np.float32)
    got = small_dft([(re[k], im[k]) for k in range(SPLIT)], 1)
    g_re = jnp.stack([v[0] for v in got])
    g_im = jnp.stack([v[1] for v in got])
    turn = 2.0 * np.pi * np.arange(SPLIT)[:, None] * np.arange(SUB)[None, :] / (2 * FR)
    c, s = np.cos(turn).astype(np.float32), np.sin(turn).astype(np.float32)
    y_re = g_re * c - g_im * s
    y_im = g_re * s + g_im * c
    l2 = np.arange(SPLIT)[:, None]
    k2 = np.arange(SPLIT // 2)[None, :]
    angle = 2.0 * np.pi * (k2 * l2 / SPLIT + l2 / (2 * SPLIT))
    extra = jnp.sum(
        np.cos(angle).astype(np.float32) * tiles[0, SPLIT // 2 :, 0][None, :]
        - np.sin(angle).astype(np.float32) * tiles[1, SPLIT // 2 :, 0][None, :],
        axis=1,
    )
    y_im = jnp.where(jnp.arange(SUB)[None, :] == 0, extra[:, None], y_im)
    l1 = np.arange(2 * SUB)[None, :]
    k1 = np.arange(SUB)[:, None]
    turn = 2.0 * np.pi * ((k1 * l1) % (2 * SUB)) / (2 * SUB)
    cos, sin = np.cos(turn), -np.sin(turn)
    sin[0, :] = 1.0 - 2.0 * (np.arange(2 * SUB) % 2)
    table = np.concatenate([cos, sin]).astype(np.float32)
    wave = jnp.dot(jnp.concatenate([y_re, y_im], axis=1), jnp.asarray(table), precision=exact)
    return wave.T.reshape(1, 2 * FR)


def exchange_kernel(blocks, x, taps, ids, x_out, taps_out, ids_out, send, recv, keep):
    me = lax.axis_index("chan")
    barrier = pltpu.get_barrier_semaphore()
    for o in range(1, blocks):
        pl.semaphore_signal(
            barrier, inc=1, device_id={"chan": lax.rem(me + o, blocks)}, device_id_type=MESH
        )
    pl.semaphore_wait(barrier, blocks - 1)
    copies = []
    for o in range(1, blocks):
        to = lax.rem(me + o, blocks)
        for z, (src, dst) in enumerate(((ids, ids_out), (taps.at[to], taps_out), (x.at[to], x_out))):
            copy = pltpu.make_async_remote_copy(
                src_ref=src,
                dst_ref=dst.at[me],
                send_sem=send.at[z, o],
                recv_sem=recv.at[z, o],
                device_id={"chan": to},
                device_id_type=MESH,
            )
            copy.start()
            copies.append(copy)
    mine = []
    for z, (src, dst) in enumerate(((ids, ids_out), (taps.at[me], taps_out), (x.at[me], x_out))):
        copy = pltpu.make_async_copy(src, dst.at[me], keep.at[z])
        copy.start()
        mine.append(copy)
    for copy in mine:
        copy.wait()
    for copy in copies:
        copy.wait()


def exchange(x, taps, ids, blocks):
    hbm = pl.BlockSpec(memory_space=pl.ANY)
    return pl.pallas_call(
        functools.partial(exchange_kernel, blocks),
        out_shape=(
            jax.ShapeDtypeStruct(x.shape, x.dtype),
            jax.ShapeDtypeStruct(taps.shape, taps.dtype),
            jax.ShapeDtypeStruct((blocks,) + ids.shape, ids.dtype),
        ),
        in_specs=[hbm] * 3,
        out_specs=(hbm,) * 3,
        scratch_shapes=[
            pltpu.SemaphoreType.DMA((3, blocks)),
            pltpu.SemaphoreType.DMA((3, blocks)),
            pltpu.SemaphoreType.DMA((3,)),
        ],
        compiler_params=pltpu.CompilerParams(collective_id=0, has_side_effects=True),
    )(x, taps, ids)


def onehot_of(all_ids, owners, blocks):
    pairs = pairs_of(blocks)
    flat = jnp.stack([all_ids[r, i] for r, i in pairs])
    nbins = owners.shape[0]
    labels = jnp.arange(nbins, dtype=jnp.int32)
    places = jnp.sum(jnp.where(flat[:, None] == labels[None, :], owners[None, :], 0), axis=1)
    hot = (places[None, :] == labels[:, None]).astype(jnp.bfloat16)
    return jnp.repeat(hot, 8, axis=1)


def split_body(traces, taps, bin_ids, owners):
    blocks = lax.axis_size("chan")
    channels = traces.shape[0]
    per = channels // blocks
    ids = jnp.broadcast_to(jnp.pad(bin_ids, ((0, 8 - ROUNDS), (0, 0))), (8, LANES))
    x, filters, all_ids = exchange(
        traces.reshape(blocks, per, FR), taps.reshape(blocks, per, taps.shape[1]), ids, blocks
    )
    onehot = onehot_of(all_ids[:, :ROUNDS, 0].T, owners, blocks)
    stack = correlate(x.reshape(channels, FR), filters.reshape(channels, taps.shape[1]), onehot, blocks)
    final = lax.psum_scatter(stack, ("chan", "hour"), scatter_dimension=0, tiled=True)
    norm = 1.0 / (FR * math.sqrt(FR * lax.axis_size("hour") * channels))
    return wave_of(final[0], norm)


def solution(mesh):
    placed = (P("chan", "hour"), P("chan", None), P(None, "chan"), P())

    def whole(traces, taps, bin_ids, owners):
        chan, hour = mesh.shape["chan"], mesh.shape["hour"]
        channels = traces.shape[0] // chan
        fits = (
            channels % (16 * chan) == 0
            and traces.shape[1] == hour * FR
            and taps.shape[1] == SPLIT * LANES // 2
            and owners.shape[0] == chan * hour
        )
        return jax.shard_map(
            split_body if fits else body,
            mesh=mesh,
            in_specs=placed,
            out_specs=P(("chan", "hour"), None),
            check_vma=False,
        )(traces, taps, bin_ids, owners)

    return whole
```

```python
import functools
import math

import jax
import jax.numpy as jnp
import numpy as np
from jax import lax
from jax.experimental import pallas as pl
from jax.experimental.pallas import tpu as pltpu
from jax.sharding import PartitionSpec as P

FR = 4096
ROUNDS = 4
MESH = pl.DeviceIdType.MESH


exact = lax.Precision.HIGHEST

def passed_along(shard, axis, by):
    devices = lax.axis_size(axis)
    pairs = [(i, i + by) for i in range(devices) if 0 <= i + by < devices]
    return lax.ppermute(shard, axis, pairs)


def transform(real_part, imag_part, count):
    span = real_part.shape[-1]
    inner = 2 * span // 128
    lead = real_part.shape[:-1]
    first = jnp.arange(64, dtype=jnp.float32)[:, None]
    middle = jnp.arange(128, dtype=jnp.float32)[None, :]
    angle_one = 2.0 * math.pi / 128.0 * jnp.mod(first * middle, 128.0)
    cos_one = jnp.cos(angle_one)
    sin_one = -jnp.sin(angle_one)
    second = jnp.arange(inner, dtype=jnp.float32)[:, None]
    angle_turn = 2.0 * math.pi / (128.0 * inner) * jnp.mod(second * middle, 128.0 * inner)
    cos_turn = jnp.cos(angle_turn)
    sin_turn = -jnp.sin(angle_turn)
    outer = jnp.arange(count // 128, dtype=jnp.float32)[None, :]
    angle_two = 2.0 * math.pi / inner * jnp.mod(second * outer, float(inner))
    cos_two = jnp.cos(angle_two)
    sin_two = -jnp.sin(angle_two)
    grid = real_part.reshape(lead + (64, inner))
    section_re = jnp.einsum("...an,ak->...nk", grid, cos_one, precision=exact)
    section_im = jnp.einsum("...an,ak->...nk", grid, sin_one, precision=exact)
    if imag_part is not None:
        grid_im = imag_part.reshape(lead + (64, inner))
        section_re = section_re - jnp.einsum("...an,ak->...nk", grid_im, sin_one, precision=exact)
        section_im = section_im + jnp.einsum("...an,ak->...nk", grid_im, cos_one, precision=exact)
    turned_re = section_re * cos_turn - section_im * sin_turn
    turned_im = section_re * sin_turn + section_im * cos_turn
    out_re = jnp.einsum("...nk,nm->...mk", turned_re, cos_two, precision=exact) - jnp.einsum(
        "...nk,nm->...mk", turned_im, sin_two, precision=exact
    )
    out_im = jnp.einsum("...nk,nm->...mk", turned_re, sin_two, precision=exact) + jnp.einsum(
        "...nk,nm->...mk", turned_im, cos_two, precision=exact
    )
    return (out_re.reshape(lead + (count,)), out_im.reshape(lead + (count,)))


def filtered(samples, filters):
    channels = samples.shape[0]
    frames = samples.shape[1] // FR
    signal = samples.astype(jnp.float32).reshape(channels, frames, FR)
    freq_re, freq_im = transform(signal, None, FR)
    padded_taps = jnp.pad(filters.astype(jnp.float32), ((0, 0), (0, FR - filters.shape[1])))
    resp_re, resp_im = transform(padded_taps, None, FR)
    resp_re = resp_re[:, None, :]
    resp_im = resp_im[:, None, :]
    spec_re = (freq_re * resp_re - freq_im * resp_im).astype(jnp.bfloat16)
    spec_im = (freq_re * resp_im + freq_im * resp_re).astype(jnp.bfloat16)
    return (spec_re, spec_im)


def body(traces, taps, bin_ids, owners):
    channels = traces.shape[0]
    frames = traces.shape[1] // FR
    spec_re, spec_im = filtered(traces, taps)
    mine = lax.axis_index("chan")
    near_re = spec_re.astype(jnp.float32)
    near_im = spec_im.astype(jnp.float32)
    results = []
    for offset in range(ROUNDS):
        far_re, far_im = passed_along((spec_re, spec_im), "chan", offset + 1)
        far_re = far_re.astype(jnp.float32)
        far_im = far_im.astype(jnp.float32)
        cross_re = jnp.sum(far_re * near_re + far_im * near_im, axis=(0, 1))
        cross_im = jnp.sum(far_im * near_re - far_re * near_im, axis=(0, 1))
        results.append(jnp.stack([cross_re, cross_im]))
    contrib = jnp.stack(results)
    nbins = owners.shape[0]
    own_bins = bin_ids[:, 0]
    labels = jnp.arange(nbins, dtype=jnp.int32)
    places = jnp.sum(jnp.where(own_bins[:, None] == labels[None, :], owners[None, :], 0), axis=1)
    valid = jnp.arange(ROUNDS, dtype=jnp.int32) < mine
    places = jnp.where(valid, places, -1)
    width = contrib.shape[2]
    flat = contrib.reshape(ROUNDS, 2 * width)
    per_device = nbins // lax.axis_size("chan")
    rows = jnp.arange(lax.axis_size("chan") * per_device, dtype=jnp.int32)
    onehot = (places[None, :] == rows[:, None]).astype(jnp.float32)
    stacked = lax.psum_scatter(
        jnp.dot(onehot, flat, precision=exact, preferred_element_type=jnp.float32),
        "chan",
        scatter_dimension=0,
        tiled=True,
    )
    stacked = stacked.reshape(per_device, 2, width)
    final = lax.psum_scatter(stacked, "hour", scatter_dimension=0, tiled=True)
    weights = jnp.where(jnp.arange(FR) == 0, 1.0, 2.0).astype(jnp.float32)
    wave_re, wave_im = transform(final[:, 0] * weights, -final[:, 1] * weights, 2 * FR)
    norm = 1.0 / (FR * math.sqrt(FR * lax.axis_size("hour") * frames * channels))
    return wave_re * norm

SPLIT = 8
SUB = FR // SPLIT
LANES = 128
TILES = SUB // LANES


def sub_tables():
    a = np.arange(SUB)[:, None]
    k1 = np.arange(SUB)[None, :]
    turn = 2.0 * np.pi * ((a * k1) % (2 * SUB)) / (2 * SUB)
    cos, sin = np.cos(turn), -np.sin(turn)
    sin[:, 0] = 1.0 - 2.0 * (np.arange(SUB) % 2)
    table = np.stack([cos.reshape(SUB, TILES, LANES), sin.reshape(SUB, TILES, LANES)], axis=2)
    return table.reshape(SUB, 2 * SUB)


def two_parts(table):
    high = table.astype(jnp.bfloat16)
    low = (table - high.astype(np.float64)).astype(jnp.bfloat16)
    return high, low


def pick_table():
    span = SPLIT * LANES
    table = np.zeros((span, span), np.float32)
    for n in range(SPLIT):
        for b in range(LANES):
            table[SPLIT * b + n, n * LANES + b] = 1.0
    return table.astype(jnp.bfloat16)


def turn_table():
    n = np.arange(SPLIT)[:, None]
    k1 = np.arange(SUB)[None, :]
    turn = 2.0 * np.pi * n * k1 / (2 * FR)
    table = np.stack([np.cos(turn), -np.sin(turn)], axis=1).reshape(SPLIT, 2, TILES, 1, LANES)
    table = np.broadcast_to(table.transpose(2, 0, 1, 3, 4), (TILES, SPLIT, 2, 8, LANES))
    return np.ascontiguousarray(table).astype(np.float32)


def times(value, angle):
    re, im = value
    c, s = math.cos(angle), math.sin(angle)
    if abs(s) < 1e-12:
        return (re, im) if c > 0 else (-re, -im)
    if abs(c) < 1e-12:
        return (-im, re) if s > 0 else (im, -re)
    if abs(abs(c) - abs(s)) < 1e-12:
        root = abs(c)
        p, q = math.copysign(1.0, c), math.copysign(1.0, s)
        first = (re if p > 0 else -re) + (-im if q > 0 else im)
        second = (re if q > 0 else -re) + (im if p > 0 else -im)
        return first * root, second * root
    return re * c - im * s, re * s + im * c


def small_dft(values, sign, half=False):
    size = len(values)
    if size == 1:
        return values
    even = small_dft(values[0::2], sign)
    odd = small_dft(values[1::2], sign)
    low, high = [], []
    for k in range(size // 2):
        turned = times(odd[k], sign * 2.0 * math.pi * k / size)
        low.append((even[k][0] + turned[0], even[k][1] + turned[1]))
        if not half:
            high.append((even[k][0] - turned[0], even[k][1] - turned[1]))
    return low + high


def pairs_of(blocks):
    return [(r, i) for r in range(ROUNDS) for i in range(blocks) if i >= r + 1]


def rows_of_pairs(ids, owners, chan, hour):
    depth = ids.shape[2]
    nbins = owners.shape[1]
    found = ids[0]
    for i in range(1, ids.shape[0]):
        found = found + ids[i]
    bins = lax.broadcasted_iota(jnp.int32, (nbins, depth), 0) + 1
    picked = (bins == found[0:1, :]).astype(jnp.float32).astype(jnp.bfloat16)
    place = lax.broadcasted_iota(jnp.int32, (nbins, nbins), 0)
    row = lax.rem(place, chan) * hour + lax.div(place, chan)
    moved = (row == owners[...]).astype(jnp.float32).astype(jnp.bfloat16)
    return jnp.dot(moved, picked, preferred_element_type=jnp.float32).astype(jnp.bfloat16)


def correlate_kernel(
    blocks, hour, x, taps, pick, high, low, turns, ids, owners, out, xd, td, fx, fh, spec, cross
):
    onehot = rows_of_pairs(ids, owners, blocks, hour)
    cross[...] = jnp.zeros_like(cross)
    rows = x.shape[0]
    per = rows // blocks
    span = SPLIT * LANES
    for q in range(FR // span):
        part = jnp.dot(
            x[:, q * span : (q + 1) * span], pick[...], preferred_element_type=jnp.float32
        ).astype(jnp.bfloat16)
        for n in range(SPLIT):
            xd[n, :, q * LANES : (q + 1) * LANES] = part[:, n * LANES : (n + 1) * LANES]
    count = taps.shape[1]
    part = jnp.dot(taps[...], pick[:count, :], preferred_element_type=jnp.float32).astype(jnp.bfloat16)
    for n in range(SPLIT):
        td[n] = part[:, n * LANES : (n + 1) * LANES]

    @pl.loop(0, SPLIT)
    def _(n):
        fx[n] = jnp.dot(xd[n], high[...], preferred_element_type=jnp.float32) + jnp.dot(
            xd[n], low[...], preferred_element_type=jnp.float32
        )
        fh[n] = jnp.dot(td[n], high[:LANES, :], preferred_element_type=jnp.float32) + jnp.dot(
            td[n], low[:LANES, :], preferred_element_type=jnp.float32
        )

    pairs = pairs_of(blocks)
    lane0 = lax.broadcasted_iota(jnp.int32, (8, LANES), 1) == 0
    for t in range(TILES):

        @pl.loop(0, rows // 8)
        def _(g):
            here = pl.ds(pl.multiple_of(8 * g, 8), 8)

            def bins_of(f):
                values, extra = [], []
                for n in range(SPLIT):
                    re = f[n, here, 2 * t * LANES : (2 * t + 1) * LANES]
                    im = f[n, here, (2 * t + 1) * LANES : (2 * t + 2) * LANES]
                    if t == 0:
                        angle = -math.pi * n / SPLIT
                        extra.append((im * math.cos(angle), im * math.sin(angle)))
                        im = jnp.where(lane0, 0.0, im)
                    if n == 0:
                        values.append((re, im))
                    else:
                        c, s = turns[t, n, 0], turns[t, n, 1]
                        values.append((re * c - im * s, re * s + im * c))
                found = small_dft(values, -1)
                if t == 0:
                    more = small_dft(extra, -1, half=True)
                    for k2 in range(SPLIT // 2):
                        old = found[SPLIT // 2 + k2]
                        found[SPLIT // 2 + k2] = tuple(
                            jnp.where(lane0, more[k2][z], old[z]) for z in range(2)
                        )
                return found

            freq = bins_of(fx)
            resp = bins_of(fh)
            for k2 in range(SPLIT):
                (xr, xi), (hr, hi) = freq[k2], resp[k2]
                spec[k2, 0, here, :] = (xr * hr - xi * hi).astype(jnp.bfloat16).astype(jnp.float32)
                spec[k2, 1, here, :] = (xr * hi + xi * hr).astype(jnp.bfloat16).astype(jnp.float32)

        @pl.loop(0, SPLIT // 2)
        def _(kk):
            both = []
            for e in range(2):
                k2 = 2 * kk + e
                for r, i in pairs:
                    p = i * ROUNDS + r
                    re = im = None
                    for c in range(per // 8):
                        near = pl.ds(i * per + 8 * c, 8)
                        far = pl.ds((i - r - 1) * per + 8 * c, 8)
                        nr, ni = spec[k2, 0, near, :], spec[k2, 1, near, :]
                        fr, fi = spec[k2, 0, far, :], spec[k2, 1, far, :]
                        one, two = fr * nr + fi * ni, fi * nr - fr * ni
                        re, im = (one, two) if re is None else (re + one, im + two)
                    cross[8 * p : 8 * p + 8, :LANES] = re
                    cross[8 * p : 8 * p + 8, LANES:] = im
                total = cross[...]
                top = total.astype(jnp.bfloat16)
                rest = (total - top.astype(jnp.float32)).astype(jnp.bfloat16)
                both.append(
                    jnp.dot(onehot, top, preferred_element_type=jnp.float32)
                    + jnp.dot(onehot, rest, preferred_element_type=jnp.float32)
                )
            for h in range(hour):
                rows_of = slice(h * blocks, (h + 1) * blocks)
                out[h, t * (SPLIT // 2) + kk] = jnp.concatenate(
                    [both[0][rows_of], both[1][rows_of]], axis=0
                ).astype(jnp.bfloat16)


def correlate(x, taps, ids, owners, hour):
    rows, blocks = x.shape[0], ids.shape[0]
    high, low = two_parts(sub_tables())
    vmem = pl.BlockSpec(memory_space=pltpu.VMEM)
    return pl.pallas_call(
        functools.partial(correlate_kernel, blocks, hour),
        out_shape=jax.ShapeDtypeStruct((hour, TILES * SPLIT // 2, 2 * blocks, 2 * LANES), jnp.bfloat16),
        in_specs=[vmem] * 8,
        out_specs=vmem,
        scratch_shapes=[
            pltpu.VMEM((SPLIT, rows, SUB), jnp.bfloat16),
            pltpu.VMEM((SPLIT, rows, LANES), jnp.bfloat16),
            pltpu.VMEM((SPLIT, rows, 2 * SUB), jnp.float32),
            pltpu.VMEM((SPLIT, rows, 2 * SUB), jnp.float32),
            pltpu.VMEM((SPLIT, 2, rows, LANES), jnp.float32),
            pltpu.VMEM((ids.shape[2], 2 * LANES), jnp.float32),
        ],
        compiler_params=pltpu.CompilerParams(vmem_limit_bytes=48 * 2**20),
    )(
        x,
        taps,
        jnp.asarray(pick_table()),
        jnp.asarray(high),
        jnp.asarray(low),
        jnp.asarray(turn_table()),
        ids,
        owners.reshape(1, -1),
    )


def mix_table():
    l2 = np.arange(SPLIT)[None, :]
    k2 = np.arange(SPLIT)[:, None]
    main = 2.0 * np.pi * k2 * l2 / SPLIT
    extra = 2.0 * np.pi * ((k2 - SPLIT // 2) * l2 / SPLIT + l2 / (2 * SPLIT))
    table = np.stack([np.cos(main), np.sin(main), np.cos(extra), np.sin(extra)])
    return np.ascontiguousarray(np.broadcast_to(table[..., None], (4, SPLIT, SPLIT, LANES))).astype(np.float32)


def back_table():
    l2 = np.arange(SPLIT)[:, None]
    turn = 2.0 * np.pi * l2 * np.arange(SUB)[None, :] / (2 * FR)
    table = np.stack([np.cos(turn), np.sin(turn)]).reshape(2, SPLIT, TILES, LANES)
    return np.ascontiguousarray(table.transpose(2, 0, 1, 3)).astype(np.float32)


def over_lanes(a, b):
    return lax.dot_general(a, b, (((1,), (1,)), ((), ())), preferred_element_type=jnp.float32)


def inverse(row, mix, back, high, low, norm):
    lane = lax.broadcasted_iota(jnp.int32, (SPLIT, LANES), 1)
    slot = lax.broadcasted_iota(jnp.int32, (SPLIT, LANES), 0)
    plain, flipped = [], []
    for t in range(TILES):
        re = row[t * SPLIT : (t + 1) * SPLIT, :LANES] * (2.0 * norm)
        im = row[t * SPLIT : (t + 1) * SPLIT, LANES:] * (2.0 * norm)
        main_re, main_im = re, im
        if t == 0:
            main_re = jnp.where(lane == 0, jnp.where(slot == 0, re * 0.5, re), re)
            drop = (lane == 0) & (slot >= SPLIT // 2)
            main_re = jnp.where(drop, 0.0, main_re)
            main_im = jnp.where(drop, 0.0, im)
        g_re = g_im = jnp.zeros((SPLIT, LANES), jnp.float32)
        for k2 in range(SPLIT):
            a, b = main_re[k2 : k2 + 1, :], main_im[k2 : k2 + 1, :]
            c, s = mix[0, k2], mix[1, k2]
            g_re = g_re + (c * a - s * b)
            g_im = g_im + (s * a + c * b)
        c, s = back[t, 0], back[t, 1]
        y_re, y_im = g_re * c - g_im * s, g_re * s + g_im * c
        if t == 0:
            more = jnp.zeros((SPLIT, LANES), jnp.float32)
            for k2 in range(SPLIT // 2, SPLIT):
                more = more + (mix[2, k2] * re[k2 : k2 + 1, :] - mix[3, k2] * im[k2 : k2 + 1, :])
            y_im = jnp.where(lane == 0, more, y_im)
        sign = jnp.where(lax.rem(lane, 2) == 0, 1.0, -1.0)
        plain += [y_re, y_im]
        flipped += [y_re * sign, y_im * sign]
    y = jnp.concatenate([jnp.concatenate(plain, axis=1), jnp.concatenate(flipped, axis=1)], axis=0)
    top = y.astype(jnp.bfloat16)
    rest = (y - top.astype(jnp.float32)).astype(jnp.bfloat16)
    return over_lanes(top, high[...]) + (over_lanes(rest, high[...]) + over_lanes(top, low[...]))


def reduce_kernel(
    chan, hour, norm, part, high, low, mix, back, out, sums, first, second, send, recv, send2, recv2
):
    mine, my_hour = lax.axis_index("chan"), lax.axis_index("hour")
    barrier = pltpu.get_barrier_semaphore()
    for o in range(1, hour):
        pl.semaphore_signal(
            barrier, inc=1, device_id={"hour": lax.rem(my_hour + o, hour)}, device_id_type=MESH
        )
    for o in range(1, chan):
        pl.semaphore_signal(
            barrier, inc=1, device_id={"chan": lax.rem(mine + o, chan)}, device_id_type=MESH
        )
    pl.semaphore_wait(barrier, chan + hour - 2)
    copies = []
    for o in range(1, hour):
        to = lax.rem(my_hour + o, hour)
        copy = pltpu.make_async_remote_copy(
            src_ref=part.at[to],
            dst_ref=first.at[o],
            send_sem=send.at[o],
            recv_sem=recv.at[o],
            device_id={"hour": to},
            device_id_type=MESH,
        )
        copy.start()
        copies.append(copy)
    width = 2 * LANES
    depth = chan * TILES * SPLIT
    total = part[my_hour].astype(jnp.float32)
    for o in range(1, hour):
        copies[o - 1].wait_recv()
        total = total + first[o].astype(jnp.float32)
    total = total.reshape(depth, width).astype(jnp.bfloat16)
    to_row = lax.broadcasted_iota(jnp.int32, (depth, depth), 0)
    from_row = lax.broadcasted_iota(jnp.int32, (depth, depth), 1)
    per = TILES * SPLIT
    wanted = lax.rem(to_row, per) * chan + lax.div(to_row, per)
    swap = (wanted == from_row).astype(jnp.float32).astype(jnp.bfloat16)
    sums[...] = jnp.dot(swap, total, preferred_element_type=jnp.float32).astype(jnp.bfloat16).reshape(sums.shape)
    later = []
    for o in range(1, chan):
        to = lax.rem(mine + o, chan)
        copy = pltpu.make_async_remote_copy(
            src_ref=sums.at[to],
            dst_ref=second.at[o],
            send_sem=send2.at[o],
            recv_sem=recv2.at[o],
            device_id={"chan": to},
            device_id_type=MESH,
        )
        copy.start()
        later.append(copy)
    row = sums[mine].astype(jnp.float32)
    for o in range(1, chan):
        later[o - 1].wait_recv()
        row = row + second[o].astype(jnp.float32)
    out[...] = inverse(row, mix, back, high, low, norm)
    for copy in copies + later:
        copy.wait_send()


def reduce(part, norm, chan, hour):
    high, low = two_parts(sub_tables())
    vmem = pl.BlockSpec(memory_space=pltpu.VMEM)
    per = TILES * SPLIT
    wave = pl.pallas_call(
        functools.partial(reduce_kernel, chan, hour, norm),
        out_shape=jax.ShapeDtypeStruct((2 * SPLIT, SUB), jnp.float32),
        in_specs=[vmem] * 5,
        out_specs=vmem,
        scratch_shapes=[
            pltpu.VMEM((chan, per, 2 * LANES), jnp.bfloat16),
            pltpu.VMEM(part.shape, part.dtype),
            pltpu.VMEM((chan, per, 2 * LANES), jnp.bfloat16),
            pltpu.SemaphoreType.DMA((hour,)),
            pltpu.SemaphoreType.DMA((hour,)),
            pltpu.SemaphoreType.DMA((chan,)),
            pltpu.SemaphoreType.DMA((chan,)),
        ],
        compiler_params=pltpu.CompilerParams(
            collective_id=1, has_side_effects=True, vmem_limit_bytes=32 * 2**20
        ),
    )(part, jnp.asarray(high), jnp.asarray(low), jnp.asarray(mix_table()), jnp.asarray(back_table()))
    return wave.reshape(2, SPLIT, SUB).transpose(0, 2, 1).reshape(1, 2 * FR)


def exchange_kernel(blocks, x, taps, bin_ids, x_out, taps_out, ids_out, ids, send, recv, keep):
    me = lax.axis_index("chan")
    place = lax.div(lax.broadcasted_iota(jnp.int32, ids.shape, 1), 8)
    labels = jnp.zeros(ids.shape, jnp.int32)
    for r in range(ROUNDS):
        live = (place == me * ROUNDS + r) & (me >= r + 1)
        labels = jnp.where(live, bin_ids[r : r + 1, :] + 1, labels)
    ids[...] = labels
    barrier = pltpu.get_barrier_semaphore()
    for o in range(1, blocks):
        pl.semaphore_signal(
            barrier, inc=1, device_id={"chan": lax.rem(me + o, blocks)}, device_id_type=MESH
        )
    pl.semaphore_wait(barrier, blocks - 1)
    copies = []
    for o in range(1, blocks):
        to = lax.rem(me + o, blocks)
        for z, (src, dst) in enumerate(((ids, ids_out), (taps.at[to], taps_out), (x.at[to], x_out))):
            copy = pltpu.make_async_remote_copy(
                src_ref=src,
                dst_ref=dst.at[me],
                send_sem=send.at[z, o],
                recv_sem=recv.at[z, o],
                device_id={"chan": to},
                device_id_type=MESH,
            )
            copy.start()
            copies.append(copy)
    mine = []
    for z, (src, dst) in enumerate(((ids, ids_out), (taps.at[me], taps_out), (x.at[me], x_out))):
        copy = pltpu.make_async_copy(src, dst.at[me], keep.at[z])
        copy.start()
        mine.append(copy)
    for copy in mine:
        copy.wait()
    for copy in copies:
        copy.wait()


def exchange(x, taps, bin_ids, blocks):
    hbm = pl.BlockSpec(memory_space=pl.ANY)
    return pl.pallas_call(
        functools.partial(exchange_kernel, blocks),
        out_shape=(
            jax.ShapeDtypeStruct(x.shape, x.dtype),
            jax.ShapeDtypeStruct(taps.shape, taps.dtype),
            jax.ShapeDtypeStruct((blocks, 8, 8 * ROUNDS * blocks), jnp.int32),
        ),
        in_specs=[hbm, hbm, pl.BlockSpec(memory_space=pltpu.VMEM)],
        out_specs=(hbm,) * 3,
        scratch_shapes=[
            pltpu.VMEM((8, 8 * ROUNDS * blocks), jnp.int32),
            pltpu.SemaphoreType.DMA((3, blocks)),
            pltpu.SemaphoreType.DMA((3, blocks)),
            pltpu.SemaphoreType.DMA((3,)),
        ],
        compiler_params=pltpu.CompilerParams(collective_id=0, has_side_effects=True),
    )(x, taps, bin_ids)


def split_body(traces, taps, bin_ids, owners):
    blocks, hour = lax.axis_size("chan"), lax.axis_size("hour")
    channels = traces.shape[0]
    per = channels // blocks
    x, filters, ids = exchange(
        traces.reshape(blocks, per, FR), taps.reshape(blocks, per, taps.shape[1]), bin_ids, blocks
    )
    part = correlate(x.reshape(channels, FR), filters.reshape(channels, taps.shape[1]), ids, owners, hour)
    norm = 1.0 / (FR * math.sqrt(FR * hour * channels))
    return reduce(part, norm, blocks, hour)


def solution(mesh):
    placed = (P("chan", "hour"), P("chan", None), P(None, "chan"), P())

    def whole(traces, taps, bin_ids, owners):
        chan, hour = mesh.shape["chan"], mesh.shape["hour"]
        channels = traces.shape[0] // chan
        fits = (
            chan == 8
            and channels % (16 * chan) == 0
            and traces.shape[1] == hour * FR
            and taps.shape[1] == SPLIT * LANES // 2
            and owners.shape[0] == chan * hour
        )
        return jax.shard_map(
            split_body if fits else body,
            mesh=mesh,
            in_specs=placed,
            out_specs=P(("chan", "hour"), None),
            check_vma=False,
        )(traces, taps, bin_ids, owners)

    return whole
```

```python
import functools
import math

import jax
import jax.numpy as jnp
import numpy as np
from jax import lax
from jax.experimental import pallas as pl
from jax.experimental.pallas import tpu as pltpu
from jax.sharding import PartitionSpec as P

FR = 4096
ROUNDS = 4
MESH = pl.DeviceIdType.MESH


exact = lax.Precision.HIGHEST

def passed_along(shard, axis, by):
    devices = lax.axis_size(axis)
    pairs = [(i, i + by) for i in range(devices) if 0 <= i + by < devices]
    return lax.ppermute(shard, axis, pairs)


def transform(real_part, imag_part, count):
    span = real_part.shape[-1]
    inner = 2 * span // 128
    lead = real_part.shape[:-1]
    first = jnp.arange(64, dtype=jnp.float32)[:, None]
    middle = jnp.arange(128, dtype=jnp.float32)[None, :]
    angle_one = 2.0 * math.pi / 128.0 * jnp.mod(first * middle, 128.0)
    cos_one = jnp.cos(angle_one)
    sin_one = -jnp.sin(angle_one)
    second = jnp.arange(inner, dtype=jnp.float32)[:, None]
    angle_turn = 2.0 * math.pi / (128.0 * inner) * jnp.mod(second * middle, 128.0 * inner)
    cos_turn = jnp.cos(angle_turn)
    sin_turn = -jnp.sin(angle_turn)
    outer = jnp.arange(count // 128, dtype=jnp.float32)[None, :]
    angle_two = 2.0 * math.pi / inner * jnp.mod(second * outer, float(inner))
    cos_two = jnp.cos(angle_two)
    sin_two = -jnp.sin(angle_two)
    grid = real_part.reshape(lead + (64, inner))
    section_re = jnp.einsum("...an,ak->...nk", grid, cos_one, precision=exact)
    section_im = jnp.einsum("...an,ak->...nk", grid, sin_one, precision=exact)
    if imag_part is not None:
        grid_im = imag_part.reshape(lead + (64, inner))
        section_re = section_re - jnp.einsum("...an,ak->...nk", grid_im, sin_one, precision=exact)
        section_im = section_im + jnp.einsum("...an,ak->...nk", grid_im, cos_one, precision=exact)
    turned_re = section_re * cos_turn - section_im * sin_turn
    turned_im = section_re * sin_turn + section_im * cos_turn
    out_re = jnp.einsum("...nk,nm->...mk", turned_re, cos_two, precision=exact) - jnp.einsum(
        "...nk,nm->...mk", turned_im, sin_two, precision=exact
    )
    out_im = jnp.einsum("...nk,nm->...mk", turned_re, sin_two, precision=exact) + jnp.einsum(
        "...nk,nm->...mk", turned_im, cos_two, precision=exact
    )
    return (out_re.reshape(lead + (count,)), out_im.reshape(lead + (count,)))


def filtered(samples, filters):
    channels = samples.shape[0]
    frames = samples.shape[1] // FR
    signal = samples.astype(jnp.float32).reshape(channels, frames, FR)
    freq_re, freq_im = transform(signal, None, FR)
    padded_taps = jnp.pad(filters.astype(jnp.float32), ((0, 0), (0, FR - filters.shape[1])))
    resp_re, resp_im = transform(padded_taps, None, FR)
    resp_re = resp_re[:, None, :]
    resp_im = resp_im[:, None, :]
    spec_re = (freq_re * resp_re - freq_im * resp_im).astype(jnp.bfloat16)
    spec_im = (freq_re * resp_im + freq_im * resp_re).astype(jnp.bfloat16)
    return (spec_re, spec_im)


def body(traces, taps, bin_ids, owners):
    channels = traces.shape[0]
    frames = traces.shape[1] // FR
    spec_re, spec_im = filtered(traces, taps)
    mine = lax.axis_index("chan")
    near_re = spec_re.astype(jnp.float32)
    near_im = spec_im.astype(jnp.float32)
    results = []
    for offset in range(ROUNDS):
        far_re, far_im = passed_along((spec_re, spec_im), "chan", offset + 1)
        far_re = far_re.astype(jnp.float32)
        far_im = far_im.astype(jnp.float32)
        cross_re = jnp.sum(far_re * near_re + far_im * near_im, axis=(0, 1))
        cross_im = jnp.sum(far_im * near_re - far_re * near_im, axis=(0, 1))
        results.append(jnp.stack([cross_re, cross_im]))
    contrib = jnp.stack(results)
    nbins = owners.shape[0]
    own_bins = bin_ids[:, 0]
    labels = jnp.arange(nbins, dtype=jnp.int32)
    places = jnp.sum(jnp.where(own_bins[:, None] == labels[None, :], owners[None, :], 0), axis=1)
    valid = jnp.arange(ROUNDS, dtype=jnp.int32) < mine
    places = jnp.where(valid, places, -1)
    width = contrib.shape[2]
    flat = contrib.reshape(ROUNDS, 2 * width)
    per_device = nbins // lax.axis_size("chan")
    rows = jnp.arange(lax.axis_size("chan") * per_device, dtype=jnp.int32)
    onehot = (places[None, :] == rows[:, None]).astype(jnp.float32)
    stacked = lax.psum_scatter(
        jnp.dot(onehot, flat, precision=exact, preferred_element_type=jnp.float32),
        "chan",
        scatter_dimension=0,
        tiled=True,
    )
    stacked = stacked.reshape(per_device, 2, width)
    final = lax.psum_scatter(stacked, "hour", scatter_dimension=0, tiled=True)
    weights = jnp.where(jnp.arange(FR) == 0, 1.0, 2.0).astype(jnp.float32)
    wave_re, wave_im = transform(final[:, 0] * weights, -final[:, 1] * weights, 2 * FR)
    norm = 1.0 / (FR * math.sqrt(FR * lax.axis_size("hour") * frames * channels))
    return wave_re * norm

SPLIT = 8
SUB = FR // SPLIT
LANES = 128
TILES = SUB // LANES


def sub_tables():
    a = np.arange(SUB)[:, None]
    k1 = np.arange(SUB)[None, :]
    turn = 2.0 * np.pi * ((a * k1) % (2 * SUB)) / (2 * SUB)
    cos, sin = np.cos(turn), -np.sin(turn)
    sin[:, 0] = 1.0 - 2.0 * (np.arange(SUB) % 2)
    table = np.stack([cos.reshape(SUB, TILES, LANES), sin.reshape(SUB, TILES, LANES)], axis=2)
    return table.reshape(SUB, 2 * SUB)


def two_parts(table):
    high = table.astype(jnp.bfloat16)
    low = (table - high.astype(np.float64)).astype(jnp.bfloat16)
    return high, low


def pick_table():
    span = SPLIT * LANES
    table = np.zeros((span, span), np.float32)
    for n in range(SPLIT):
        for b in range(LANES):
            table[SPLIT * b + n, n * LANES + b] = 1.0
    return table.astype(jnp.bfloat16)


def turn_table():
    n = np.arange(SPLIT)[:, None]
    k1 = np.arange(SUB)[None, :]
    turn = 2.0 * np.pi * n * k1 / (2 * FR)
    table = np.stack([np.cos(turn), -np.sin(turn)], axis=1).reshape(SPLIT, 2, TILES, 1, LANES)
    table = np.broadcast_to(table.transpose(2, 0, 1, 3, 4), (TILES, SPLIT, 2, 8, LANES))
    return np.ascontiguousarray(table).astype(np.float32)


def times(value, angle):
    re, im = value
    c, s = math.cos(angle), math.sin(angle)
    if abs(s) < 1e-12:
        return (re, im) if c > 0 else (-re, -im)
    if abs(c) < 1e-12:
        return (-im, re) if s > 0 else (im, -re)
    if abs(abs(c) - abs(s)) < 1e-12:
        root = abs(c)
        p, q = math.copysign(1.0, c), math.copysign(1.0, s)
        first = (re if p > 0 else -re) + (-im if q > 0 else im)
        second = (re if q > 0 else -re) + (im if p > 0 else -im)
        return first * root, second * root
    return re * c - im * s, re * s + im * c


def small_dft(values, sign, half=False):
    size = len(values)
    if size == 1:
        return values
    even = small_dft(values[0::2], sign)
    odd = small_dft(values[1::2], sign)
    low, high = [], []
    for k in range(size // 2):
        turned = times(odd[k], sign * 2.0 * math.pi * k / size)
        low.append((even[k][0] + turned[0], even[k][1] + turned[1]))
        if not half:
            high.append((even[k][0] - turned[0], even[k][1] - turned[1]))
    return low + high


def pairs_of(blocks):
    return [(r, i) for r in range(ROUNDS) for i in range(blocks) if i >= r + 1]


def rows_of_pairs(ids, owners, chan, hour):
    depth = ids.shape[1]
    nbins = owners.shape[1]
    bins = lax.broadcasted_iota(jnp.int32, (nbins, depth), 0) + 1
    picked = (bins == ids[0:1, :]).astype(jnp.float32).astype(jnp.bfloat16)
    place = lax.broadcasted_iota(jnp.int32, (nbins, nbins), 0)
    row = lax.rem(place, chan) * hour + lax.div(place, chan)
    moved = (row == owners[...]).astype(jnp.float32).astype(jnp.bfloat16)
    return jnp.dot(moved, picked, preferred_element_type=jnp.float32).astype(jnp.bfloat16)


def mix_table():
    l2 = np.arange(SPLIT)[None, :]
    k2 = np.arange(SPLIT)[:, None]
    main = 2.0 * np.pi * k2 * l2 / SPLIT
    extra = 2.0 * np.pi * ((k2 - SPLIT // 2) * l2 / SPLIT + l2 / (2 * SPLIT))
    table = np.stack([np.cos(main), np.sin(main), np.cos(extra), np.sin(extra)])
    return np.ascontiguousarray(np.broadcast_to(table[..., None], (4, SPLIT, SPLIT, LANES))).astype(np.float32)


def back_table():
    l2 = np.arange(SPLIT)[:, None]
    turn = 2.0 * np.pi * l2 * np.arange(SUB)[None, :] / (2 * FR)
    table = np.stack([np.cos(turn), np.sin(turn)]).reshape(2, SPLIT, TILES, LANES)
    return np.ascontiguousarray(table.transpose(2, 0, 1, 3)).astype(np.float32)


def over_lanes(a, b):
    return lax.dot_general(a, b, (((1,), (1,)), ((), ())), preferred_element_type=jnp.float32)


def inverse(row, mix, back, high, low, norm):
    lane = lax.broadcasted_iota(jnp.int32, (SPLIT, LANES), 1)
    slot = lax.broadcasted_iota(jnp.int32, (SPLIT, LANES), 0)
    plain, flipped = [], []
    for t in range(TILES):
        re = row[t * SPLIT : (t + 1) * SPLIT, :LANES] * (2.0 * norm)
        im = row[t * SPLIT : (t + 1) * SPLIT, LANES:] * (2.0 * norm)
        main_re, main_im = re, im
        if t == 0:
            main_re = jnp.where(lane == 0, jnp.where(slot == 0, re * 0.5, re), re)
            drop = (lane == 0) & (slot >= SPLIT // 2)
            main_re = jnp.where(drop, 0.0, main_re)
            main_im = jnp.where(drop, 0.0, im)
        g_re = g_im = jnp.zeros((SPLIT, LANES), jnp.float32)
        for k2 in range(SPLIT):
            a, b = main_re[k2 : k2 + 1, :], main_im[k2 : k2 + 1, :]
            c, s = mix[0, k2], mix[1, k2]
            g_re = g_re + (c * a - s * b)
            g_im = g_im + (s * a + c * b)
        c, s = back[t, 0], back[t, 1]
        y_re, y_im = g_re * c - g_im * s, g_re * s + g_im * c
        if t == 0:
            more = jnp.zeros((SPLIT, LANES), jnp.float32)
            for k2 in range(SPLIT // 2, SPLIT):
                more = more + (mix[2, k2] * re[k2 : k2 + 1, :] - mix[3, k2] * im[k2 : k2 + 1, :])
            y_im = jnp.where(lane == 0, more, y_im)
        sign = jnp.where(lax.rem(lane, 2) == 0, 1.0, -1.0)
        plain += [y_re, y_im]
        flipped += [y_re * sign, y_im * sign]
    y = jnp.concatenate([jnp.concatenate(plain, axis=1), jnp.concatenate(flipped, axis=1)], axis=0)
    top = y.astype(jnp.bfloat16)
    rest = (y - top.astype(jnp.float32)).astype(jnp.bfloat16)
    return over_lanes(top, high[...]) + (over_lanes(rest, high[...]) + over_lanes(top, low[...]))


def kernel(chan, hour, norm, x, taps, bin_ids, owners, *refs):
    tables, out = refs[:6], refs[6]
    held = refs[7:13]
    pick, high, low, turns, mix, back = held
    xin, tin, ids, ids_in, xd, td, fx, fh, spec, cross, part, first, sums, second = refs[13:27]
    table_sem, own_sem, ids_send, ids_recv, t_send, t_recv, x_send, x_recv = refs[27:35]
    f_send, f_recv, send, recv, send2, recv2 = refs[35:]
    me, my_hour = lax.axis_index("chan"), lax.axis_index("hour")
    per = xin.shape[1]
    span = SPLIT * LANES
    share = pl.ds(pl.multiple_of(my_hour * (tin.shape[2] // hour), LANES), tin.shape[2] // hour)

    def partner(o):
        to, bit = me, 1
        while bit < chan:
            to = to + lax.rem(lax.div(o, bit), 2) * bit * (1 - 2 * lax.rem(lax.div(me, bit), 2))
            bit *= 2
        return to

    def sent(src, dst, sends, recvs, **device):
        return pltpu.make_async_remote_copy(
            src_ref=src, dst_ref=dst, send_sem=sends, recv_sem=recvs, device_id=device, device_id_type=MESH
        )

    loads = [pltpu.make_async_copy(src, dst, table_sem.at[z]) for z, (src, dst) in enumerate(zip(tables, held))]
    own = [
        pltpu.make_async_copy(x.at[me], xin.at[me], own_sem.at[0]),
        pltpu.make_async_copy(taps.at[me, :, share], tin.at[me, :, share], own_sem.at[1]),
    ]
    for copy in own + loads:
        copy.start()
    barrier = pltpu.get_barrier_semaphore()
    for o in range(1, hour):
        pl.semaphore_signal(
            barrier, inc=1, device_id={"hour": lax.rem(my_hour + o, hour)}, device_id_type=MESH
        )
    for o in range(1, chan):
        pl.semaphore_signal(barrier, inc=1, device_id={"chan": partner(o)}, device_id_type=MESH)
    place = lax.div(lax.broadcasted_iota(jnp.int32, ids.shape, 1), 8)
    labels = jnp.zeros(ids.shape, jnp.int32)
    for r in range(ROUNDS):
        live = (place == me * ROUNDS + r) & (me >= r + 1)
        labels = jnp.where(live, bin_ids[:, r : r + 1] + 1, labels)
    ids[...] = labels
    pl.semaphore_wait(barrier, chan + hour - 2)

    def x_copy(o):
        to = partner(o)
        return sent(x.at[to], xin.at[me], x_send.at[o], x_recv.at[o], chan=to)

    far_first = sorted(range(1, chan), key=lambda o: -(o.bit_length()))
    tap_copies, id_copies = [], []
    for o in far_first:
        to = partner(o)
        tap_copies.append(
            sent(taps.at[to, :, share], tin.at[me, :, share], t_send.at[o], t_recv.at[o], chan=to)
        )
        tap_copies[-1].start()
        x_copy(o).start()
    for o in far_first:
        id_copies.append(sent(ids, ids_in.at[o], ids_send.at[o], ids_recv.at[o], chan=partner(o)))
        id_copies[-1].start()
    for copy in own + loads:
        copy.wait()

    def take(block):
        rows = pl.ds(pl.multiple_of(block * per, per), per)
        flat = jnp.concatenate([xin[block, :, q * span : (q + 1) * span] for q in range(FR // span)], axis=0)
        got = jnp.dot(flat, pick[...], preferred_element_type=jnp.float32).astype(jnp.bfloat16)
        for q in range(FR // span):
            for n in range(SPLIT):
                xd[n * per : (n + 1) * per, q * LANES : (q + 1) * LANES] = got[
                    q * per : (q + 1) * per, n * LANES : (n + 1) * LANES
                ]
        found = jnp.dot(xd[...], high[...], preferred_element_type=jnp.float32) + jnp.dot(
            xd[...], low[...], preferred_element_type=jnp.float32
        )
        for n in range(SPLIT):
            fx[n, rows, :] = found[n * per : (n + 1) * per]

    take(me)
    for copy in tap_copies:
        copy.wait_recv()
    forwards = []
    for o in range(1, hour):
        to = lax.rem(my_hour + o, hour)
        forwards.append(sent(tin.at[:, :, share], tin.at[:, :, share], f_send.at[o], f_recv.at[o], hour=to))
        forwards[-1].start()

    @pl.loop(1, chan // 2)
    def _(o):
        x_copy(o).wait_recv()
        take(partner(o))

    for copy in forwards:
        copy.wait_recv()
    count = tin.shape[2]
    got = jnp.dot(
        tin[...].reshape(chan * per, count), pick[:count, :], preferred_element_type=jnp.float32
    ).astype(jnp.bfloat16)
    for n in range(SPLIT):
        td[n] = got[:, n * LANES : (n + 1) * LANES]

    @pl.loop(0, SPLIT)
    def _(n):
        fh[n] = jnp.dot(td[n], high[:LANES, :], preferred_element_type=jnp.float32) + jnp.dot(
            td[n], low[:LANES, :], preferred_element_type=jnp.float32
        )

    for copy in id_copies:
        copy.wait_recv()
    labels = ids[...]
    for o in range(1, chan):
        labels = labels + ids_in[o]
    onehot = rows_of_pairs(labels, owners, chan, hour)
    cross[...] = jnp.zeros_like(cross)

    @pl.loop(chan // 2, chan)
    def _(o):
        x_copy(o).wait_recv()
        take(partner(o))

    pairs = pairs_of(chan)
    lane0 = lax.broadcasted_iota(jnp.int32, (8, LANES), 1) == 0
    steps = SPLIT // 2

    def part_copy(t, o):
        to = lax.rem(my_hour + o, hour)
        where = pl.ds(t * steps, steps)
        return sent(part.at[to, where], first.at[o, where], send.at[t, o], recv.at[t, o], hour=to)

    def tile(t, edge):
        @pl.loop(0, chan * per // 8)
        def _(g):
            here = pl.ds(pl.multiple_of(8 * g, 8), 8)

            def bins_of(f):
                values, extra = [], []
                for n in range(SPLIT):
                    re = f[n, here, pl.ds(pl.multiple_of(2 * t * LANES, LANES), LANES)]
                    im = f[n, here, pl.ds(pl.multiple_of((2 * t + 1) * LANES, LANES), LANES)]
                    if edge:
                        angle = -math.pi * n / SPLIT
                        extra.append((im * math.cos(angle), im * math.sin(angle)))
                        im = jnp.where(lane0, 0.0, im)
                    if n == 0:
                        values.append((re, im))
                    else:
                        c, s = turns[t, n, 0], turns[t, n, 1]
                        values.append((re * c - im * s, re * s + im * c))
                found = small_dft(values, -1)
                if edge:
                    more = small_dft(extra, -1, half=True)
                    for k2 in range(SPLIT // 2):
                        old = found[SPLIT // 2 + k2]
                        found[SPLIT // 2 + k2] = tuple(
                            jnp.where(lane0, more[k2][z], old[z]) for z in range(2)
                        )
                return found

            freq = bins_of(fx)
            resp = bins_of(fh)
            for k2 in range(SPLIT):
                (xr, xi), (hr, hi) = freq[k2], resp[k2]
                spec[k2, 0, here, :] = (xr * hr - xi * hi).astype(jnp.bfloat16).astype(jnp.float32)
                spec[k2, 1, here, :] = (xr * hi + xi * hr).astype(jnp.bfloat16).astype(jnp.float32)

        @pl.loop(0, steps)
        def _(kk):
            both = []
            for e in range(2):
                k2 = 2 * kk + e
                for r, i in pairs:
                    p = i * ROUNDS + r
                    re = im = None
                    for c in range(per // 8):
                        near = pl.ds(i * per + 8 * c, 8)
                        far = pl.ds((i - r - 1) * per + 8 * c, 8)
                        nr, ni = spec[k2, 0, near, :], spec[k2, 1, near, :]
                        fr, fi = spec[k2, 0, far, :], spec[k2, 1, far, :]
                        one, two = fr * nr + fi * ni, fi * nr - fr * ni
                        re, im = (one, two) if re is None else (re + one, im + two)
                    cross[8 * p : 8 * p + 8, :LANES] = re
                    cross[8 * p : 8 * p + 8, LANES:] = im
                total = cross[...]
                top = total.astype(jnp.bfloat16)
                rest = (total - top.astype(jnp.float32)).astype(jnp.bfloat16)
                both.append(
                    jnp.dot(onehot, top, preferred_element_type=jnp.float32)
                    + jnp.dot(onehot, rest, preferred_element_type=jnp.float32)
                )
            for h in range(hour):
                rows_of = slice(h * chan, (h + 1) * chan)
                part[h, t * steps + kk] = jnp.concatenate(
                    [both[0][rows_of], both[1][rows_of]], axis=0
                ).astype(jnp.bfloat16)

        for o in range(1, hour):
            part_copy(t, o).start()

    tile(0, True)

    @pl.loop(1, TILES)
    def _(t):
        tile(t, False)

    width = 2 * LANES
    depth = chan * TILES * SPLIT
    for t in range(TILES):
        for o in range(1, hour):
            part_copy(t, o).wait_recv()
    total = part[my_hour].astype(jnp.float32)
    for o in range(1, hour):
        total = total + first[o].astype(jnp.float32)
    total = total.reshape(depth, width).astype(jnp.bfloat16)
    to_row = lax.broadcasted_iota(jnp.int32, (depth, depth), 0)
    from_row = lax.broadcasted_iota(jnp.int32, (depth, depth), 1)
    slots = TILES * SPLIT
    wanted = lax.rem(to_row, slots) * chan + lax.div(to_row, slots)
    swap = (wanted == from_row).astype(jnp.float32).astype(jnp.bfloat16)
    sums[...] = jnp.dot(swap, total, preferred_element_type=jnp.float32).astype(jnp.bfloat16).reshape(sums.shape)
    later = []
    for o in far_first:
        to = partner(o)
        later.append(sent(sums.at[to], second.at[o], send2.at[o], recv2.at[o], chan=to))
        later[-1].start()
    row = sums[me].astype(jnp.float32)
    for copy in later:
        copy.wait_recv()
    for o in range(1, chan):
        row = row + second[o].astype(jnp.float32)
    out[...] = inverse(row, mix, back, high, low, norm)
    for copy in tap_copies + id_copies + forwards + later:
        copy.wait_send()
    for o in range(1, chan):
        x_copy(o).wait_send()
    for t in range(TILES):
        for o in range(1, hour):
            part_copy(t, o).wait_send()


def split_body(traces, taps, bin_ids, owners):
    chan, hour = lax.axis_size("chan"), lax.axis_size("hour")
    channels, count = taps.shape
    per = channels // chan
    norm = 1.0 / (FR * math.sqrt(FR * hour * channels))
    high, low = two_parts(sub_tables())
    tables = [pick_table(), high, low, turn_table(), mix_table(), back_table()]
    depth = 8 * ROUNDS * chan
    slots = TILES * SPLIT
    part = (hour, slots // 2, 2 * chan, 2 * LANES)
    sums = (chan, slots, 2 * LANES)
    vmem, hbm = pl.BlockSpec(memory_space=pltpu.VMEM), pl.BlockSpec(memory_space=pl.ANY)
    sems = pltpu.SemaphoreType.DMA
    wave = pl.pallas_call(
        functools.partial(kernel, chan, hour, norm),
        out_shape=jax.ShapeDtypeStruct((2 * SPLIT, SUB), jnp.float32),
        in_specs=[hbm, hbm, vmem, vmem] + [hbm] * len(tables),
        out_specs=vmem,
        scratch_shapes=[pltpu.VMEM(table.shape, table.dtype) for table in tables]
        + [
            pltpu.VMEM((chan, per, FR), jnp.bfloat16),
            pltpu.VMEM((chan, per, count), jnp.bfloat16),
            pltpu.VMEM((8, depth), jnp.int32),
            pltpu.VMEM((chan, 8, depth), jnp.int32),
            pltpu.VMEM((SPLIT * per, SUB), jnp.bfloat16),
            pltpu.VMEM((SPLIT, channels, LANES), jnp.bfloat16),
            pltpu.VMEM((SPLIT, channels, 2 * SUB), jnp.float32),
            pltpu.VMEM((SPLIT, channels, 2 * SUB), jnp.float32),
            pltpu.VMEM((SPLIT, 2, channels, LANES), jnp.float32),
            pltpu.VMEM((depth, 2 * LANES), jnp.float32),
            pltpu.VMEM(part, jnp.bfloat16),
            pltpu.VMEM(part, jnp.bfloat16),
            pltpu.VMEM(sums, jnp.bfloat16),
            pltpu.VMEM(sums, jnp.bfloat16),
            sems((len(tables),)),
            sems((2,)),
        ]
        + [sems((chan,))] * 6
        + [sems((hour,))] * 2
        + [sems((TILES, hour))] * 2
        + [sems((chan,))] * 2,
        compiler_params=pltpu.CompilerParams(
            collective_id=0, has_side_effects=True, vmem_limit_bytes=56 * 2**20
        ),
    )(
        traces.reshape(chan, per, FR),
        taps.reshape(chan, per, count),
        bin_ids.T,
        owners.reshape(1, -1),
        *[jnp.asarray(table) for table in tables],
    )
    return wave.reshape(2, SPLIT, SUB).transpose(0, 2, 1).reshape(1, 2 * FR)


def solution(mesh):
    placed = (P("chan", "hour"), P("chan", None), P(None, "chan"), P())

    def whole(traces, taps, bin_ids, owners):
        chan, hour = mesh.shape["chan"], mesh.shape["hour"]
        channels = traces.shape[0] // chan
        fits = (
            chan == 8
            and channels % (16 * chan) == 0
            and traces.shape[1] == hour * FR
            and taps.shape[1] == SPLIT * LANES // 2
            and owners.shape[0] == chan * hour
        )
        return jax.shard_map(
            split_body if fits else body,
            mesh=mesh,
            in_specs=placed,
            out_specs=P(("chan", "hour"), None),
            check_vma=False,
        )(traces, taps, bin_ids, owners)

    return whole
```

```python
import functools
import math

import jax
import jax.numpy as jnp
import numpy as np
from jax import lax
from jax.experimental import pallas as pl
from jax.experimental.pallas import tpu as pltpu
from jax.sharding import PartitionSpec as P

FR = 4096
ROUNDS = 4
MESH = pl.DeviceIdType.MESH


exact = lax.Precision.HIGHEST

def passed_along(shard, axis, by):
    devices = lax.axis_size(axis)
    pairs = [(i, i + by) for i in range(devices) if 0 <= i + by < devices]
    return lax.ppermute(shard, axis, pairs)


def transform(real_part, imag_part, count):
    span = real_part.shape[-1]
    inner = 2 * span // 128
    lead = real_part.shape[:-1]
    first = jnp.arange(64, dtype=jnp.float32)[:, None]
    middle = jnp.arange(128, dtype=jnp.float32)[None, :]
    angle_one = 2.0 * math.pi / 128.0 * jnp.mod(first * middle, 128.0)
    cos_one = jnp.cos(angle_one)
    sin_one = -jnp.sin(angle_one)
    second = jnp.arange(inner, dtype=jnp.float32)[:, None]
    angle_turn = 2.0 * math.pi / (128.0 * inner) * jnp.mod(second * middle, 128.0 * inner)
    cos_turn = jnp.cos(angle_turn)
    sin_turn = -jnp.sin(angle_turn)
    outer = jnp.arange(count // 128, dtype=jnp.float32)[None, :]
    angle_two = 2.0 * math.pi / inner * jnp.mod(second * outer, float(inner))
    cos_two = jnp.cos(angle_two)
    sin_two = -jnp.sin(angle_two)
    grid = real_part.reshape(lead + (64, inner))
    section_re = jnp.einsum("...an,ak->...nk", grid, cos_one, precision=exact)
    section_im = jnp.einsum("...an,ak->...nk", grid, sin_one, precision=exact)
    if imag_part is not None:
        grid_im = imag_part.reshape(lead + (64, inner))
        section_re = section_re - jnp.einsum("...an,ak->...nk", grid_im, sin_one, precision=exact)
        section_im = section_im + jnp.einsum("...an,ak->...nk", grid_im, cos_one, precision=exact)
    turned_re = section_re * cos_turn - section_im * sin_turn
    turned_im = section_re * sin_turn + section_im * cos_turn
    out_re = jnp.einsum("...nk,nm->...mk", turned_re, cos_two, precision=exact) - jnp.einsum(
        "...nk,nm->...mk", turned_im, sin_two, precision=exact
    )
    out_im = jnp.einsum("...nk,nm->...mk", turned_re, sin_two, precision=exact) + jnp.einsum(
        "...nk,nm->...mk", turned_im, cos_two, precision=exact
    )
    return (out_re.reshape(lead + (count,)), out_im.reshape(lead + (count,)))


def filtered(samples, filters):
    channels = samples.shape[0]
    frames = samples.shape[1] // FR
    signal = samples.astype(jnp.float32).reshape(channels, frames, FR)
    freq_re, freq_im = transform(signal, None, FR)
    padded_taps = jnp.pad(filters.astype(jnp.float32), ((0, 0), (0, FR - filters.shape[1])))
    resp_re, resp_im = transform(padded_taps, None, FR)
    resp_re = resp_re[:, None, :]
    resp_im = resp_im[:, None, :]
    spec_re = (freq_re * resp_re - freq_im * resp_im).astype(jnp.bfloat16)
    spec_im = (freq_re * resp_im + freq_im * resp_re).astype(jnp.bfloat16)
    return (spec_re, spec_im)


def body(traces, taps, bin_ids, owners):
    channels = traces.shape[0]
    frames = traces.shape[1] // FR
    spec_re, spec_im = filtered(traces, taps)
    mine = lax.axis_index("chan")
    near_re = spec_re.astype(jnp.float32)
    near_im = spec_im.astype(jnp.float32)
    results = []
    for offset in range(ROUNDS):
        far_re, far_im = passed_along((spec_re, spec_im), "chan", offset + 1)
        far_re = far_re.astype(jnp.float32)
        far_im = far_im.astype(jnp.float32)
        cross_re = jnp.sum(far_re * near_re + far_im * near_im, axis=(0, 1))
        cross_im = jnp.sum(far_im * near_re - far_re * near_im, axis=(0, 1))
        results.append(jnp.stack([cross_re, cross_im]))
    contrib = jnp.stack(results)
    nbins = owners.shape[0]
    own_bins = bin_ids[:, 0]
    labels = jnp.arange(nbins, dtype=jnp.int32)
    places = jnp.sum(jnp.where(own_bins[:, None] == labels[None, :], owners[None, :], 0), axis=1)
    valid = jnp.arange(ROUNDS, dtype=jnp.int32) < mine
    places = jnp.where(valid, places, -1)
    width = contrib.shape[2]
    flat = contrib.reshape(ROUNDS, 2 * width)
    per_device = nbins // lax.axis_size("chan")
    rows = jnp.arange(lax.axis_size("chan") * per_device, dtype=jnp.int32)
    onehot = (places[None, :] == rows[:, None]).astype(jnp.float32)
    stacked = lax.psum_scatter(
        jnp.dot(onehot, flat, precision=exact, preferred_element_type=jnp.float32),
        "chan",
        scatter_dimension=0,
        tiled=True,
    )
    stacked = stacked.reshape(per_device, 2, width)
    final = lax.psum_scatter(stacked, "hour", scatter_dimension=0, tiled=True)
    weights = jnp.where(jnp.arange(FR) == 0, 1.0, 2.0).astype(jnp.float32)
    wave_re, wave_im = transform(final[:, 0] * weights, -final[:, 1] * weights, 2 * FR)
    norm = 1.0 / (FR * math.sqrt(FR * lax.axis_size("hour") * frames * channels))
    return wave_re * norm

SPLIT = 8
SUB = FR // SPLIT
LANES = 128
TILES = SUB // LANES


def sub_tables():
    a = np.arange(SUB)[:, None]
    k1 = np.arange(SUB)[None, :]
    turn = 2.0 * np.pi * ((a * k1) % (2 * SUB)) / (2 * SUB)
    cos, sin = np.cos(turn), -np.sin(turn)
    sin[:, 0] = 1.0 - 2.0 * (np.arange(SUB) % 2)
    table = np.stack([cos.reshape(SUB, TILES, LANES), sin.reshape(SUB, TILES, LANES)], axis=2)
    return table.reshape(SUB, 2 * SUB)


def two_parts(table):
    high = table.astype(jnp.bfloat16)
    low = (table - high.astype(np.float64)).astype(jnp.bfloat16)
    return high, low


def pick_table():
    span = SPLIT * LANES
    table = np.zeros((span, span), np.float32)
    for n in range(SPLIT):
        for b in range(LANES):
            table[SPLIT * b + n, n * LANES + b] = 1.0
    return table.astype(jnp.bfloat16)


def turn_table():
    n = np.arange(SPLIT)[:, None]
    k1 = np.arange(SUB)[None, :]
    turn = 2.0 * np.pi * n * k1 / (2 * FR)
    table = np.stack([np.cos(turn), -np.sin(turn)], axis=1).reshape(SPLIT, 2, TILES, 1, LANES)
    table = np.broadcast_to(table.transpose(2, 0, 1, 3, 4), (TILES, SPLIT, 2, 8, LANES))
    return np.ascontiguousarray(table).astype(np.float32)


def times(value, angle):
    re, im = value
    c, s = math.cos(angle), math.sin(angle)
    if abs(s) < 1e-12:
        return (re, im) if c > 0 else (-re, -im)
    if abs(c) < 1e-12:
        return (-im, re) if s > 0 else (im, -re)
    if abs(abs(c) - abs(s)) < 1e-12:
        root = abs(c)
        p, q = math.copysign(1.0, c), math.copysign(1.0, s)
        first = (re if p > 0 else -re) + (-im if q > 0 else im)
        second = (re if q > 0 else -re) + (im if p > 0 else -im)
        return first * root, second * root
    return re * c - im * s, re * s + im * c


def small_dft(values, sign, half=False):
    size = len(values)
    if size == 1:
        return values
    even = small_dft(values[0::2], sign)
    odd = small_dft(values[1::2], sign)
    low, high = [], []
    for k in range(size // 2):
        turned = times(odd[k], sign * 2.0 * math.pi * k / size)
        low.append((even[k][0] + turned[0], even[k][1] + turned[1]))
        if not half:
            high.append((even[k][0] - turned[0], even[k][1] - turned[1]))
    return low + high


def pairs_of(blocks):
    return [(r, i) for r in range(ROUNDS) for i in range(blocks) if i >= r + 1]


def rows_of_pairs(ids, owners, chan, hour):
    depth = ids.shape[1]
    nbins = owners.shape[1]
    bins = lax.broadcasted_iota(jnp.int32, (nbins, depth), 0) + 1
    picked = (bins == ids[0:1, :]).astype(jnp.float32).astype(jnp.bfloat16)
    place = lax.broadcasted_iota(jnp.int32, (nbins, nbins), 0)
    row = lax.rem(place, chan) * hour + lax.div(place, chan)
    moved = (row == owners[...]).astype(jnp.float32).astype(jnp.bfloat16)
    return jnp.dot(moved, picked, preferred_element_type=jnp.float32).astype(jnp.bfloat16)


def mix_table():
    l2 = np.arange(SPLIT)[None, :]
    k2 = np.arange(SPLIT)[:, None]
    main = 2.0 * np.pi * k2 * l2 / SPLIT
    extra = 2.0 * np.pi * ((k2 - SPLIT // 2) * l2 / SPLIT + l2 / (2 * SPLIT))
    table = np.stack([np.cos(main), np.sin(main), np.cos(extra), np.sin(extra)])
    return np.ascontiguousarray(np.broadcast_to(table[..., None], (4, SPLIT, SPLIT, LANES))).astype(np.float32)


def back_table():
    l2 = np.arange(SPLIT)[:, None]
    turn = 2.0 * np.pi * l2 * np.arange(SUB)[None, :] / (2 * FR)
    table = np.stack([np.cos(turn), np.sin(turn)]).reshape(2, SPLIT, TILES, LANES)
    return np.ascontiguousarray(table.transpose(2, 0, 1, 3)).astype(np.float32)


def over_lanes(a, b):
    return lax.dot_general(a, b, (((1,), (1,)), ((), ())), preferred_element_type=jnp.float32)


def inverse(row, mix, back, high, low, norm):
    lane = lax.broadcasted_iota(jnp.int32, (SPLIT, LANES), 1)
    slot = lax.broadcasted_iota(jnp.int32, (SPLIT, LANES), 0)
    plain, flipped = [], []
    for t in range(TILES):
        re = row[t * SPLIT : (t + 1) * SPLIT, :LANES] * (2.0 * norm)
        im = row[t * SPLIT : (t + 1) * SPLIT, LANES:] * (2.0 * norm)
        main_re, main_im = re, im
        if t == 0:
            main_re = jnp.where(lane == 0, jnp.where(slot == 0, re * 0.5, re), re)
            drop = (lane == 0) & (slot >= SPLIT // 2)
            main_re = jnp.where(drop, 0.0, main_re)
            main_im = jnp.where(drop, 0.0, im)
        g_re = g_im = jnp.zeros((SPLIT, LANES), jnp.float32)
        for k2 in range(SPLIT):
            a, b = main_re[k2 : k2 + 1, :], main_im[k2 : k2 + 1, :]
            c, s = mix[0, k2], mix[1, k2]
            g_re = g_re + (c * a - s * b)
            g_im = g_im + (s * a + c * b)
        c, s = back[t, 0], back[t, 1]
        y_re, y_im = g_re * c - g_im * s, g_re * s + g_im * c
        if t == 0:
            more = jnp.zeros((SPLIT, LANES), jnp.float32)
            for k2 in range(SPLIT // 2, SPLIT):
                more = more + (mix[2, k2] * re[k2 : k2 + 1, :] - mix[3, k2] * im[k2 : k2 + 1, :])
            y_im = jnp.where(lane == 0, more, y_im)
        sign = jnp.where(lax.rem(lane, 2) == 0, 1.0, -1.0)
        plain += [y_re, y_im]
        flipped += [y_re * sign, y_im * sign]
    y = jnp.concatenate([jnp.concatenate(plain, axis=1), jnp.concatenate(flipped, axis=1)], axis=0)
    top = y.astype(jnp.bfloat16)
    rest = (y - top.astype(jnp.float32)).astype(jnp.bfloat16)
    return over_lanes(top, high[...]) + (over_lanes(rest, high[...]) + over_lanes(top, low[...]))


def kernel(chan, hour, norm, x, taps, bin_ids, owners, *refs):
    tables, out = refs[:6], refs[6]
    held = refs[7:13]
    pick, high, low, turns, mix, back = held
    xin, tin, ids, ids_in, xd, td, fx, fh, spec, cross, part, first, sums, second = refs[13:27]
    table_sem, own_sem, ids_send, ids_recv, t_send, t_recv, x_send, x_recv = refs[27:35]
    f_send, f_recv, send, recv, send2, recv2 = refs[35:]
    me, my_hour = lax.axis_index("chan"), lax.axis_index("hour")
    per = xin.shape[1]
    span = SPLIT * LANES
    share = pl.ds(pl.multiple_of(my_hour * (tin.shape[2] // hour), LANES), tin.shape[2] // hour)

    def partner(o):
        to, bit = me, 1
        while bit < chan:
            to = to + lax.rem(lax.div(o, bit), 2) * bit * (1 - 2 * lax.rem(lax.div(me, bit), 2))
            bit *= 2
        return to

    def sent(src, dst, sends, recvs, **device):
        return pltpu.make_async_remote_copy(
            src_ref=src, dst_ref=dst, send_sem=sends, recv_sem=recvs, device_id=device, device_id_type=MESH
        )

    loads = [pltpu.make_async_copy(src, dst, table_sem.at[z]) for z, (src, dst) in enumerate(zip(tables, held))]
    own = [
        pltpu.make_async_copy(x.at[me], xin.at[me], own_sem.at[0]),
        pltpu.make_async_copy(taps.at[me, :, share], tin.at[me, :, share], own_sem.at[1]),
    ]
    for copy in own + loads:
        copy.start()
    barrier = pltpu.get_barrier_semaphore()
    for o in range(1, hour):
        pl.semaphore_signal(
            barrier, inc=1, device_id={"hour": lax.rem(my_hour + o, hour)}, device_id_type=MESH
        )
    for o in range(1, chan):
        pl.semaphore_signal(barrier, inc=1, device_id={"chan": partner(o)}, device_id_type=MESH)
    place = lax.div(lax.broadcasted_iota(jnp.int32, ids.shape, 1), 8)
    labels = jnp.zeros(ids.shape, jnp.int32)
    for r in range(ROUNDS):
        live = (place == me * ROUNDS + r) & (me >= r + 1)
        labels = jnp.where(live, bin_ids[:, r : r + 1] + 1, labels)
    ids[...] = labels
    pl.semaphore_wait(barrier, chan + hour - 2)

    def x_copy(o):
        to = partner(o)
        return sent(x.at[to], xin.at[me], x_send.at[o], x_recv.at[o], chan=to)

    far_first = sorted(range(1, chan), key=lambda o: -(o.bit_length()))
    tap_copies, id_copies = [], []
    for o in far_first:
        to = partner(o)
        tap_copies.append(
            sent(taps.at[to, :, share], tin.at[me, :, share], t_send.at[o], t_recv.at[o], chan=to)
        )
        tap_copies[-1].start()
    for o in far_first:
        id_copies.append(sent(ids, ids_in.at[o], ids_send.at[o], ids_recv.at[o], chan=partner(o)))
        id_copies[-1].start()
    for o in range(1, chan):
        x_copy(o).start()
    own[1].wait()
    for copy in tap_copies:
        copy.wait_recv()
    forwards = []
    for o in range(1, hour):
        to = lax.rem(my_hour + o, hour)
        forwards.append(sent(tin.at[:, :, share], tin.at[:, :, share], f_send.at[o], f_recv.at[o], hour=to))
        forwards[-1].start()
    for copy in loads + own[:1]:
        copy.wait()

    lane0 = lax.broadcasted_iota(jnp.int32, (8, LANES), 1) == 0

    def spectra(block, t, edge):
        @pl.loop(0, per // 8)
        def _(g):
            piece = pl.ds(pl.multiple_of(8 * g, 8), 8)
            here = pl.ds(pl.multiple_of(block * per + 8 * g, 8), 8)

            def bins_of(f, rows):
                values, extra = [], []
                for n in range(SPLIT):
                    re = f[n, rows, pl.ds(pl.multiple_of(2 * t * LANES, LANES), LANES)]
                    im = f[n, rows, pl.ds(pl.multiple_of((2 * t + 1) * LANES, LANES), LANES)]
                    if edge:
                        angle = -math.pi * n / SPLIT
                        extra.append((im * math.cos(angle), im * math.sin(angle)))
                        im = jnp.where(lane0, 0.0, im)
                    if n == 0:
                        values.append((re, im))
                    else:
                        c, s = turns[t, n, 0], turns[t, n, 1]
                        values.append((re * c - im * s, re * s + im * c))
                found = small_dft(values, -1)
                if edge:
                    more = small_dft(extra, -1, half=True)
                    for k2 in range(SPLIT // 2):
                        old = found[SPLIT // 2 + k2]
                        found[SPLIT // 2 + k2] = tuple(
                            jnp.where(lane0, more[k2][z], old[z]) for z in range(2)
                        )
                return found

            freq = bins_of(fx, piece)
            resp = bins_of(fh, here)
            for k2 in range(SPLIT):
                (xr, xi), (hr, hi) = freq[k2], resp[k2]
                spec[t, k2, 0, here, :] = (xr * hr - xi * hi).astype(jnp.bfloat16).astype(jnp.float32)
                spec[t, k2, 1, here, :] = (xr * hi + xi * hr).astype(jnp.bfloat16).astype(jnp.float32)

    def take(block):
        flat = jnp.concatenate([xin[block, :, q * span : (q + 1) * span] for q in range(FR // span)], axis=0)
        got = jnp.dot(flat, pick[...], preferred_element_type=jnp.float32).astype(jnp.bfloat16)
        for q in range(FR // span):
            for n in range(SPLIT):
                xd[n * per : (n + 1) * per, q * LANES : (q + 1) * LANES] = got[
                    q * per : (q + 1) * per, n * LANES : (n + 1) * LANES
                ]
        found = jnp.dot(xd[...], high[...], preferred_element_type=jnp.float32) + jnp.dot(
            xd[...], low[...], preferred_element_type=jnp.float32
        )
        for n in range(SPLIT):
            fx[n] = found[n * per : (n + 1) * per]
        spectra(block, 0, True)

        @pl.loop(1, TILES)
        def _(t):
            spectra(block, t, False)

    for copy in forwards:
        copy.wait_recv()
    count = tin.shape[2]
    got = jnp.dot(
        tin[...].reshape(chan * per, count), pick[:count, :], preferred_element_type=jnp.float32
    ).astype(jnp.bfloat16)
    for n in range(SPLIT):
        td[n] = got[:, n * LANES : (n + 1) * LANES]

    @pl.loop(0, SPLIT)
    def _(n):
        fh[n] = jnp.dot(td[n], high[:LANES, :], preferred_element_type=jnp.float32) + jnp.dot(
            td[n], low[:LANES, :], preferred_element_type=jnp.float32
        )

    for copy in id_copies:
        copy.wait_recv()
    labels = ids[...]
    for o in range(1, chan):
        labels = labels + ids_in[o]
    onehot = rows_of_pairs(labels, owners, chan, hour)
    cross[...] = jnp.zeros_like(cross)

    take(me)

    @pl.loop(1, chan // 2)
    def _(o):
        x_copy(o).wait_recv()
        take(partner(o))

    @pl.loop(chan // 2, chan)
    def _(o):
        x_copy(o).wait_recv()
        take(partner(o))

    pairs = pairs_of(chan)
    steps = SPLIT // 2

    def part_copy(t, o):
        to = lax.rem(my_hour + o, hour)
        where = pl.ds(t * steps, steps)
        return sent(part.at[to, where], first.at[o, where], send.at[t, o], recv.at[t, o], hour=to)

    @pl.loop(0, TILES)
    def _(t):
        @pl.loop(0, steps)
        def _(kk):
            both = []
            for e in range(2):
                k2 = 2 * kk + e
                for r, i in pairs:
                    p = i * ROUNDS + r
                    re = im = None
                    for c in range(per // 8):
                        near = pl.ds(i * per + 8 * c, 8)
                        far = pl.ds((i - r - 1) * per + 8 * c, 8)
                        nr, ni = spec[t, k2, 0, near, :], spec[t, k2, 1, near, :]
                        fr, fi = spec[t, k2, 0, far, :], spec[t, k2, 1, far, :]
                        one, two = fr * nr + fi * ni, fi * nr - fr * ni
                        re, im = (one, two) if re is None else (re + one, im + two)
                    cross[8 * p : 8 * p + 8, :LANES] = re
                    cross[8 * p : 8 * p + 8, LANES:] = im
                total = cross[...]
                top = total.astype(jnp.bfloat16)
                rest = (total - top.astype(jnp.float32)).astype(jnp.bfloat16)
                both.append(
                    jnp.dot(onehot, top, preferred_element_type=jnp.float32)
                    + jnp.dot(onehot, rest, preferred_element_type=jnp.float32)
                )
            for h in range(hour):
                rows_of = slice(h * chan, (h + 1) * chan)
                part[h, t * steps + kk] = jnp.concatenate(
                    [both[0][rows_of], both[1][rows_of]], axis=0
                ).astype(jnp.bfloat16)

        for o in range(1, hour):
            part_copy(t, o).start()

    width = 2 * LANES
    depth = chan * TILES * SPLIT
    for t in range(TILES):
        for o in range(1, hour):
            part_copy(t, o).wait_recv()
    total = part[my_hour].astype(jnp.float32)
    for o in range(1, hour):
        total = total + first[o].astype(jnp.float32)
    total = total.reshape(depth, width).astype(jnp.bfloat16)
    to_row = lax.broadcasted_iota(jnp.int32, (depth, depth), 0)
    from_row = lax.broadcasted_iota(jnp.int32, (depth, depth), 1)
    slots = TILES * SPLIT
    wanted = lax.rem(to_row, slots) * chan + lax.div(to_row, slots)
    swap = (wanted == from_row).astype(jnp.float32).astype(jnp.bfloat16)
    sums[...] = jnp.dot(swap, total, preferred_element_type=jnp.float32).astype(jnp.bfloat16).reshape(sums.shape)
    later = []
    for o in far_first:
        to = partner(o)
        later.append(sent(sums.at[to], second.at[o], send2.at[o], recv2.at[o], chan=to))
        later[-1].start()
    row = sums[me].astype(jnp.float32)
    for copy in later:
        copy.wait_recv()
    for o in range(1, chan):
        row = row + second[o].astype(jnp.float32)
    out[...] = inverse(row, mix, back, high, low, norm)
    for copy in tap_copies + id_copies + forwards + later:
        copy.wait_send()
    for o in range(1, chan):
        x_copy(o).wait_send()
    for t in range(TILES):
        for o in range(1, hour):
            part_copy(t, o).wait_send()


def split_body(traces, taps, bin_ids, owners):
    chan, hour = lax.axis_size("chan"), lax.axis_size("hour")
    channels, count = taps.shape
    per = channels // chan
    norm = 1.0 / (FR * math.sqrt(FR * hour * channels))
    high, low = two_parts(sub_tables())
    tables = [pick_table(), high, low, turn_table(), mix_table(), back_table()]
    depth = 8 * ROUNDS * chan
    slots = TILES * SPLIT
    part = (hour, slots // 2, 2 * chan, 2 * LANES)
    sums = (chan, slots, 2 * LANES)
    vmem, hbm = pl.BlockSpec(memory_space=pltpu.VMEM), pl.BlockSpec(memory_space=pl.ANY)
    sems = pltpu.SemaphoreType.DMA
    wave = pl.pallas_call(
        functools.partial(kernel, chan, hour, norm),
        out_shape=jax.ShapeDtypeStruct((2 * SPLIT, SUB), jnp.float32),
        in_specs=[hbm, hbm, vmem, vmem] + [hbm] * len(tables),
        out_specs=vmem,
        scratch_shapes=[pltpu.VMEM(table.shape, table.dtype) for table in tables]
        + [
            pltpu.VMEM((chan, per, FR), jnp.bfloat16),
            pltpu.VMEM((chan, per, count), jnp.bfloat16),
            pltpu.VMEM((8, depth), jnp.int32),
            pltpu.VMEM((chan, 8, depth), jnp.int32),
            pltpu.VMEM((SPLIT * per, SUB), jnp.bfloat16),
            pltpu.VMEM((SPLIT, channels, LANES), jnp.bfloat16),
            pltpu.VMEM((SPLIT, per, 2 * SUB), jnp.float32),
            pltpu.VMEM((SPLIT, channels, 2 * SUB), jnp.float32),
            pltpu.VMEM((TILES, SPLIT, 2, channels, LANES), jnp.float32),
            pltpu.VMEM((depth, 2 * LANES), jnp.float32),
            pltpu.VMEM(part, jnp.bfloat16),
            pltpu.VMEM(part, jnp.bfloat16),
            pltpu.VMEM(sums, jnp.bfloat16),
            pltpu.VMEM(sums, jnp.bfloat16),
            sems((len(tables),)),
            sems((2,)),
        ]
        + [sems((chan,))] * 6
        + [sems((hour,))] * 2
        + [sems((TILES, hour))] * 2
        + [sems((chan,))] * 2,
        compiler_params=pltpu.CompilerParams(
            collective_id=0, has_side_effects=True, vmem_limit_bytes=56 * 2**20
        ),
    )(
        traces.reshape(chan, per, FR),
        taps.reshape(chan, per, count),
        bin_ids.T,
        owners.reshape(1, -1),
        *[jnp.asarray(table) for table in tables],
    )
    return wave.reshape(2, SPLIT, SUB).transpose(0, 2, 1).reshape(1, 2 * FR)


def solution(mesh):
    placed = (P("chan", "hour"), P("chan", None), P(None, "chan"), P())

    def whole(traces, taps, bin_ids, owners):
        chan, hour = mesh.shape["chan"], mesh.shape["hour"]
        channels = traces.shape[0] // chan
        fits = (
            chan == 8
            and channels % (16 * chan) == 0
            and traces.shape[1] == hour * FR
            and taps.shape[1] == SPLIT * LANES // 2
            and owners.shape[0] == chan * hour
        )
        return jax.shard_map(
            split_body if fits else body,
            mesh=mesh,
            in_specs=placed,
            out_specs=P(("chan", "hour"), None),
            check_vma=False,
        )(traces, taps, bin_ids, owners)

    return whole
```
